32 devices in a mesh: row: 4 (over y, x), col: 8 (over z, core).
Axes of the slice: x: 2, y: 2, z: 4, core: 2. Of those that a mesh axis runs over, the one named last changes fastest.
Arguments:
- iterate: float32 [128, 1024], P('row', 'col'), may hold values from 0 to 2
- gradient: float32 [128, 1024], P('row', 'col'), may hold values from -6 to 6
- dual_coeffs: float32 [8, 7, 128, 1024], P(None, None, 'row', 'col'), may hold values from -3 to 3
- weights: float32 [8, 7], replicated, may hold values from 0.2 to 2
Outputs:
- new_image: float32 [128, 1024], P('row', 'col')
- new_duals: float32 [8, 7, 128, 1024], P(None, None, 'row', 'col')
The draws below stay inside these ranges and needn't reach their ends.
All inputs are finite; a program needn't handle non-finite values.
Results may differ from the reference program's by a relative error of at most 0.0001.
Values sent between devices are 32-bit elements; how exact they have to be, the bound alone decides.
A program may use at most 64 MiB of HBM per device.

```python
import math
import jax
import jax.numpy as jnp
import numpy as np
from jax import lax

BASES = 8
LEVELS = 2
BANDS = 7
NR = 128
NC = 1024


def steps_of(stream_key, dims, cuts, low, largest):
    def one(dim, shards_of):
        heights = jax.random.uniform(jax.random.fold_in(jax.random.fold_in(stream_key, 6), dim), (shards_of,), jnp.float32, low / len(cuts), largest / len(cuts))
        return jnp.repeat(jnp.exp(heights), dims[dim] // shards_of).reshape((-1,) + (1,) * (len(dims) - dim - 1))

    gain = one(*cuts[0])
    for cut in cuts[1:]:
        gain = gain * one(*cut)
    return gain


def centred(rng, dims, spread, most, shards=(), kind=jnp.bfloat16):
    values = spread * jax.random.normal(rng, dims, jnp.float32)
    if shards:
        values = values * steps_of(rng, dims, shards, -0.22, 0.18)
    return jnp.clip(values, -most, most).astype(kind)


def setup_inputs(seed: int = 0) -> dict:
    key_of = jax.random.split(jax.random.key(seed), 5)
    iterate = jnp.clip(2.0 * jax.random.uniform(key_of[0], (NR, NC), jnp.float32) ** steps_of(key_of[0], (NR, NC), ((0, 4), (1, 8)), -0.2, 0.2), 0.0, 2.0)
    gradient = centred(key_of[1], (NR, NC), 1.0, 6.0, ((0, 4), (1, 8)), jnp.float32)
    dual_coeffs = centred(key_of[2], (BASES, BANDS, NR, NC), 0.5, 3.0, ((2, 4), (3, 8)), jnp.float32)
    weights = jnp.clip(jnp.exp(jax.random.uniform(key_of[3], (BASES, BANDS), jnp.float32, math.log(0.2), math.log(2.0))), 0.2, 2.0)
    return dict(iterate=iterate, gradient=gradient, dual_coeffs=dual_coeffs, weights=weights)


primal_step = 0.5
daubechies_table = [[0.7071067811865476, 0.7071067811865476], [0.48296291314469025, 0.836516303737469, 0.22414386804185735, -0.12940952255092145], [0.3326705529509569, 0.8068915093133388, 0.4598775021193313, -0.13501102001039084, -0.08544127388224149, 0.035226291882100656], [0.23037781330885523, 0.7148465705525415, 0.6308807679295904, -0.02798376941698385, -0.18703481171888114, 0.030841381835986965, 0.032883011666982945, -0.010597401784997278], [0.160102397974125, 0.6038292697974729, 0.7243085284385744, 0.13842814590110342, -0.24229488706619015, -0.03224486958502952, 0.07757149384006515, -0.006241490213011705, -0.012580751999015526, 0.003335725285001549], [0.11154074335008017, 0.4946238903983854, 0.7511339080215775, 0.3152503517092432, -0.22626469396516913, -0.12976686756709563, 0.09750160558707936, 0.02752286553001629, -0.031582039318031156, 0.0005538422009938016, 0.004777257511010651, -0.00107730108499558], [0.07785205408506236, 0.39653931948230575, 0.7291320908465551, 0.4697822874053586, -0.14390600392910627, -0.22403618499416572, 0.07130921926705004, 0.0806126091510659, -0.03802993693503463, -0.01657454163101562, 0.012550998556013784, 0.00042957797300470274, -0.0018016407039998328, 0.0003537138000010399], [0.05441584224308161, 0.3128715909144659, 0.6756307362980128, 0.5853546836548691, -0.015829105256023893, -0.2840155429624281, 0.00047248457399797254, 0.128747426620186, -0.01736930100202211, -0.04408825393106472, 0.013981027917015516, 0.008746094047015655, -0.00487035299301066, -0.0003917403729959771, 0.0006754494059985568, -0.00011747678400228192]]

def tap_tables():
    low_table = np.zeros((BASES, 16))
    high_table = np.zeros((BASES, 16))
    for basis_index in range(BASES):
        taps = np.array(daubechies_table[basis_index])
        low_taps = taps * math.sqrt(2.0) / np.sum(taps) / math.sqrt(2.0)
        length = len(low_taps)
        half_len = length // 2
        for position in range(length):
            low_table[basis_index, position - half_len + 8] = low_taps[position]
            high_table[basis_index, position - half_len + 8] = (-1.0) ** position * low_taps[length - 1 - position]
    return (jnp.asarray(low_table, jnp.float32), jnp.asarray(high_table, jnp.float32))

def periodic_axis(signal, taps, dilation, axis_pos, direction):
    result = None
    for position in range(16):
        shifted = jnp.roll(signal, -direction * dilation * (position - 8), axis=axis_pos)
        weighted = taps[:, position][:, None, None] * shifted
        result = weighted if result is None else result + weighted
    return result

def synth_level(approx, details, low_taps, high_taps, dilation):
    col_low = periodic_axis(approx, low_taps, dilation, 2, -1) + periodic_axis(details[1], high_taps, dilation, 2, -1)
    col_high = periodic_axis(details[0], low_taps, dilation, 2, -1) + periodic_axis(details[2], high_taps, dilation, 2, -1)
    return periodic_axis(col_low, low_taps, dilation, 1, -1) + periodic_axis(col_high, high_taps, dilation, 1, -1)

def analyse(signal, low_taps, high_taps):
    approx = jnp.broadcast_to(signal[None], (BASES,) + signal.shape)
    bands_list = []
    for level_index in range(LEVELS):
        dilation = 2 ** level_index
        low_rows = periodic_axis(approx, low_taps, dilation, 1, 1)
        high_rows = periodic_axis(approx, high_taps, dilation, 1, 1)
        bands_list.append(periodic_axis(high_rows, low_taps, dilation, 2, 1))
        bands_list.append(periodic_axis(low_rows, high_taps, dilation, 2, 1))
        bands_list.append(periodic_axis(high_rows, high_taps, dilation, 2, 1))
        approx = periodic_axis(low_rows, low_taps, dilation, 2, 1)
    bands_list.append(approx)
    return jnp.stack(bands_list, axis=1)

def reference(iterate, gradient, dual_coeffs, weights):
    low_taps, high_taps = tap_tables()
    frame_scale = 1.0 / math.sqrt(BASES)
    approx = dual_coeffs[:, 3 * LEVELS]
    for level_index in reversed(range(LEVELS)):
        details = [dual_coeffs[:, 3 * level_index + part_index] for part_index in range(3)]
        approx = synth_level(approx, details, low_taps, high_taps, 2 ** level_index)
    synth_total = lax.optimization_barrier(jnp.sum(approx, axis=0))
    new_image = jnp.maximum(iterate - primal_step * (gradient + frame_scale * synth_total), 0.0)
    extrapolated = 2.0 * new_image - iterate
    coeffs = frame_scale * analyse(extrapolated, low_taps, high_taps)
    bound_all = weights[:, :, None, None]
    return (new_image, jnp.clip(dual_coeffs + coeffs, -bound_all, bound_all))
```

```python
import functools
import math

import jax
import jax.numpy as jnp
import ml_dtypes
import numpy as np
from jax import lax
from jax.experimental import pallas as pl
from jax.experimental.pallas import tpu as pltpu
from jax.sharding import PartitionSpec as P

BASES = 8
BANDS = 7
REACH = 24
MESH = pl.DeviceIdType.MESH

primal_step = 0.5

daubechies_table = [
    [0.7071067811865476, 0.7071067811865476],
    [0.48296291314469025, 0.836516303737469, 0.22414386804185735, -0.12940952255092145],
    [
        0.3326705529509569,
        0.8068915093133388,
        0.4598775021193313,
        -0.13501102001039084,
        -0.08544127388224149,
        0.035226291882100656,
    ],
    [
        0.23037781330885523,
        0.7148465705525415,
        0.6308807679295904,
        -0.02798376941698385,
        -0.18703481171888114,
        0.030841381835986965,
        0.032883011666982945,
        -0.010597401784997278,
    ],
    [
        0.160102397974125,
        0.6038292697974729,
        0.7243085284385744,
        0.13842814590110342,
        -0.24229488706619015,
        -0.03224486958502952,
        0.07757149384006515,
        -0.006241490213011705,
        -0.012580751999015526,
        0.003335725285001549,
    ],
    [
        0.11154074335008017,
        0.4946238903983854,
        0.7511339080215775,
        0.3152503517092432,
        -0.22626469396516913,
        -0.12976686756709563,
        0.09750160558707936,
        0.02752286553001629,
        -0.031582039318031156,
        0.0005538422009938016,
        0.004777257511010651,
        -0.00107730108499558,
    ],
    [
        0.07785205408506236,
        0.39653931948230575,
        0.7291320908465551,
        0.4697822874053586,
        -0.14390600392910627,
        -0.22403618499416572,
        0.07130921926705004,
        0.0806126091510659,
        -0.03802993693503463,
        -0.01657454163101562,
        0.012550998556013784,
        0.00042957797300470274,
        -0.0018016407039998328,
        0.0003537138000010399,
    ],
    [
        0.05441584224308161,
        0.3128715909144659,
        0.6756307362980128,
        0.5853546836548691,
        -0.015829105256023893,
        -0.2840155429624281,
        0.00047248457399797254,
        0.128747426620186,
        -0.01736930100202211,
        -0.04408825393106472,
        0.013981027917015516,
        0.008746094047015655,
        -0.00487035299301066,
        -0.0003917403729959771,
        0.0006754494059985568,
        -0.00011747678400228192,
    ],
]


def tap_pairs(basis):
    taps = np.array(daubechies_table[basis])
    low = taps / np.sum(taps)
    high = np.array([(-1.0) ** t * low[len(low) - 1 - t] for t in range(len(low))])
    return low, high


def composite(basis):
    low, high = tap_pairs(basis)
    n = len(low) // 2
    fine = [{t - n: f[t] for t in range(2 * n)} for f in (low, high)]
    both = []
    for f in (low, high):
        out = {}
        for s in range(2 * n):
            for t in range(2 * n):
                off = (s - n) + 2 * (t - n)
                out[off] = out.get(off, 0.0) + low[s] * f[t]
        both.append(out)
    return fine + both


def halves(matrix):
    high = matrix.astype(np.float32).astype(ml_dtypes.bfloat16)
    low = (matrix - high.astype(np.float64)).astype(np.float32).astype(ml_dtypes.bfloat16)
    return np.stack([high, low])


@functools.lru_cache(maxsize=None)
def matrices(h, w):
    span = h + 2 * REACH
    scale = 1.0 / math.sqrt(BASES)
    a = np.zeros((BASES, 4 * span, BANDS * h))
    b = np.zeros((BASES, BANDS * h, 2 * span))
    c = np.zeros((BASES, 4 * w, 2 * w))
    kinds = [(1, 0), (0, 1), (1, 1), (3, 2), (2, 3), (3, 3), (2, 2)]
    for basis in range(BASES):
        filters = composite(basis)
        rows = np.zeros((4, h, span))
        for kind in range(4):
            for off, tap in filters[kind].items():
                for j in range(h):
                    rows[kind, j, j + REACH + off] += scale * tap
                for j in range(w):
                    c[basis, kind * w + j, (j + off) % (2 * w)] += tap
        for band, (row_kind, col_kind) in enumerate(kinds):
            mat = rows[row_kind]
            a[basis, col_kind * span : (col_kind + 1) * span, band * h : (band + 1) * h] = mat.T
            at = col_kind % 2
            b[basis, band * h : (band + 1) * h, at * span : (at + 1) * span] = mat
    return halves(a), halves(b), halves(c)


def split(x):
    high = x.astype(jnp.bfloat16)
    low = (x - high.astype(jnp.float32)).astype(jnp.bfloat16)
    return high, low


def left_dot(m_high, m_low, x):
    width = x.shape[1]
    high, low = split(x)
    pair = jnp.dot(
        m_high, jnp.concatenate([high, low], axis=1), preferred_element_type=jnp.float32
    )
    rest = jnp.dot(m_low, high, preferred_element_type=jnp.float32)
    return pair[:, :width] + (pair[:, width:] + rest)


def synth_one(x, a_ref, c_ref, h, w):
    span = h + 2 * REACH
    z = left_dot(a_ref[0, 0], a_ref[1, 0], x)
    z = jnp.concatenate([z[k * span : (k + 1) * span] for k in range(4)], axis=1)
    high, low = split(z)
    pair = jnp.dot(
        jnp.concatenate([high, low], axis=0), c_ref[0, 0], preferred_element_type=jnp.float32
    )
    rest = jnp.dot(high, c_ref[1, 0], preferred_element_type=jnp.float32)
    return pair[:span] + (pair[span:] + rest)


def partners():
    return [(dr, dc) for dr in (-2, -1, 0, 1, 2) for dc in (-1, 0, 1) if (dr, dc) != (0, 0)]


def near():
    return [(dr, dc) for dr in (-1, 0, 1) for dc in (-1, 0, 1) if (dr, dc) != (0, 0)]


def overlap(dr, h):
    span = h + 2 * REACH
    shift = h * abs(dr)
    return (shift, 0, span - shift) if dr > 0 else (0, shift, span - shift)


def border(dr, h):
    if dr == 0:
        return (REACH, REACH, h)
    return (h, 0, REACH) if dr > 0 else (REACH, h + REACH, REACH)


def primal_kernel(
    it_ref, gr_ref, x_ref, a_ref, c_ref, e_ref, img_ref,
    acc, held, slots, side, sides_in, bar_sent, bar_recv, send, recv,
):
    h, w = it_ref.shape
    span = h + 2 * REACH
    step = pl.program_id(0)
    nrow, ncol = lax.axis_size("row"), lax.axis_size("col")
    row, col = lax.axis_index("row"), lax.axis_index("col")

    def device(dr, dc):
        return (lax.rem(row + dr + 2 * nrow, nrow), lax.rem(col + dc + ncol, ncol))

    def held_copy(i, dr, dc):
        here, there, rows = border(dr, h)
        return pltpu.make_async_remote_copy(
            src_ref=held.at[1, pl.ds(here, rows)],
            dst_ref=held.at[1 + dc if dc else 3, pl.ds(there, rows)],
            send_sem=bar_sent.at[i], recv_sem=bar_recv.at[i],
            device_id=device(dr, dc), device_id_type=MESH,
        )

    def sum_copy(i, dr, dc):
        here, there, rows = overlap(dr, h)
        slot = dr + 2
        if dc == 0:
            src = acc.at[pl.ds(here, rows)]
            dst = slots.at[slot, pl.ds(there, rows)]
        else:
            src = side.at[(dc + 1) // 2, pl.ds(here, rows)]
            dst = sides_in.at[(dc + 1) // 2, slot, pl.ds(there, rows)]
        return pltpu.make_async_remote_copy(
            src_ref=src, dst_ref=dst, send_sem=send.at[i], recv_sem=recv.at[i],
            device_id=device(dr, dc), device_id_type=MESH,
        )

    @pl.when(step == 0)
    def _():
        barrier = pltpu.get_barrier_semaphore()
        for dr, dc in partners():
            pl.semaphore_signal(barrier, inc=1, device_id=device(dr, dc), device_id_type=MESH)
        held[1, REACH : REACH + h] = it_ref[...]
        acc[...] = jnp.zeros_like(acc)
        acc[REACH : REACH + h, :w] = it_ref[...] - primal_step * gr_ref[...]
        pl.semaphore_wait(barrier, len(partners()))
        for i, (dr, dc) in enumerate(near()):
            held_copy(i, dr, dc).start()

    acc[...] += -primal_step * synth_one(x_ref[0], a_ref, c_ref, h, w)

    @pl.when(step == BASES - 1)
    def _():
        left = lax.broadcasted_iota(jnp.int32, (span, w), 1) < w // 2
        mine, over = acc[:, :w], acc[:, w:]
        side[0] = jnp.where(left, mine, over)
        side[1] = jnp.where(left, over, mine)
        for i, (dr, dc) in enumerate(partners()):
            sum_copy(i, dr, dc).start()
        for i, (dr, dc) in enumerate(near()):
            held_copy(i, dr, dc).wait()
        for i, (dr, dc) in enumerate(partners()):
            sum_copy(i, dr, dc).wait()

        def gather(read, start):
            total = start
            for dr in (-2, -1, 0, 1, 2):
                if dr == 0 and start is not None:
                    continue
                _, there, rows = overlap(dr, h)
                part = read(dr + 2, there, rows)
                sizes = (there, span - there - rows)
                above, below = [jnp.zeros((n, part.shape[1]), jnp.float32) for n in sizes]
                blocks = [above] * (there > 0) + [part] + [below] * (sizes[1] > 0)
                part = jnp.concatenate(blocks, axis=0) if len(blocks) > 1 else part
                total = part if total is None else total + part
            return total

        mid = gather(lambda s, t, n: slots[s, t : t + n], acc[...])
        from_right = gather(lambda s, t, n: sides_in[0, s, t : t + n], None)
        from_left = gather(lambda s, t, n: sides_in[1, s, t : t + n], None)
        inner = mid[:, :w] + jnp.where(left, from_left, from_right)
        outer = mid[:, w:] + jnp.where(left, from_right, from_left)
        inner = jnp.maximum(inner, 0.0)
        outer = jnp.maximum(outer, 0.0)
        img_ref[...] = inner[REACH : REACH + h]
        it_inner = jnp.concatenate(
            [held[3, :REACH], held[1, REACH : REACH + h], held[3, REACH + h :]], axis=0
        )
        it_outer = jnp.where(left, held[0], held[2])
        ext = jnp.concatenate([2.0 * inner - it_inner, 2.0 * outer - it_outer], axis=1)
        high, low = split(ext)
        e_ref[:span] = high
        e_ref[span:] = low


def dual_kernel(wt_ref, e_ref, img_ref, x_ref, b_ref, c_ref, img_out, x_out):
    h, w = img_ref.shape
    span = h + 2 * REACH
    step = pl.program_id(0)

    @pl.when(step == 0)
    def _():
        img_out[...] = img_ref[...]

    across = (((1,), (1,)), ((), ()))
    pair = lax.dot_general(e_ref[...], c_ref[0, 0], across, preferred_element_type=jnp.float32)
    rest = lax.dot_general(
        e_ref[:span], c_ref[1, 0], across, preferred_element_type=jnp.float32
    )
    z = pair[:span] + (pair[span:] + rest)
    for first, last, at in ((0, 3, 0), (3, 7, 2)):
        data = jnp.concatenate(
            [z[:, at * w : (at + 1) * w], z[:, (at + 1) * w : (at + 2) * w]], axis=0
        )
        rows = slice(first * h, last * h)
        coeffs = left_dot(b_ref[0, 0, rows], b_ref[1, 0, rows], data)
        for band in range(first, last):
            bound = wt_ref[step, band]
            value = x_ref[0, band * h : (band + 1) * h]
            value = value + coeffs[(band - first) * h : (band - first + 1) * h]
            x_out[0, band * h : (band + 1) * h] = jnp.clip(value, -bound, bound)


def on_device(iterate, gradient, dual_coeffs, weights):
    h, w = iterate.shape
    span = h + 2 * REACH
    a, b, c = [jnp.asarray(m) for m in matrices(h, w)]
    duals = dual_coeffs.reshape(BASES, BANDS * h, w)
    whole = pl.BlockSpec((h, w), lambda i: (0, 0))
    per_basis = pl.BlockSpec((1, BANDS * h, w), lambda i: (i, 0, 0))
    halved = lambda m: pl.BlockSpec((2, 1) + m.shape[2:], lambda i: (0, i, 0, 0))
    ext, image = pl.pallas_call(
        primal_kernel,
        grid=(BASES,),
        out_shape=(
            jax.ShapeDtypeStruct((2 * span, 2 * w), jnp.bfloat16),
            jax.ShapeDtypeStruct((h, w), jnp.float32),
        ),
        in_specs=[whole, whole, per_basis, halved(a), halved(c)],
        out_specs=(pl.BlockSpec((2 * span, 2 * w), lambda i: (0, 0)), whole),
        scratch_shapes=[
            pltpu.VMEM((span, 2 * w), jnp.float32),
            pltpu.VMEM((4, span, w), jnp.float32),
            pltpu.VMEM((5, span, 2 * w), jnp.float32),
            pltpu.VMEM((2, span, w), jnp.float32),
            pltpu.VMEM((2, 5, span, w), jnp.float32),
            pltpu.SemaphoreType.DMA((8,)),
            pltpu.SemaphoreType.DMA((8,)),
            pltpu.SemaphoreType.DMA((14,)),
            pltpu.SemaphoreType.DMA((14,)),
        ],
        compiler_params=pltpu.CompilerParams(
            collective_id=0, has_side_effects=True, vmem_limit_bytes=24 * 2**20
        ),
    )(iterate, gradient, duals, a, c)
    new_image, new_duals = pl.pallas_call(
        dual_kernel,
        grid=(BASES,),
        out_shape=(
            jax.ShapeDtypeStruct((h, w), jnp.float32),
            jax.ShapeDtypeStruct(duals.shape, jnp.float32),
        ),
        in_specs=[
            pl.BlockSpec(memory_space=pltpu.SMEM),
            pl.BlockSpec((2 * span, 2 * w), lambda i: (0, 0)),
            whole,
            per_basis,
            halved(b),
            halved(c),
        ],
        out_specs=(whole, per_basis),
        compiler_params=pltpu.CompilerParams(vmem_limit_bytes=24 * 2**20),
    )(weights, ext, image, duals, b, c)
    return new_image, new_duals.reshape(dual_coeffs.shape)


def solution(mesh):
    return jax.shard_map(
        on_device,
        mesh=mesh,
        in_specs=(P("row", "col"), P("row", "col"), P(None, None, "row", "col"), P()),
        out_specs=(P("row", "col"), P(None, None, "row", "col")),
        check_vma=False,
    )
```

```python
import functools
import math

import jax
import jax.numpy as jnp
import ml_dtypes
import numpy as np
from jax import lax
from jax.experimental import pallas as pl
from jax.experimental.pallas import tpu as pltpu
from jax.sharding import PartitionSpec as P

BASES = 8
BANDS = 7
REACH = 24
GROUP = 2
VMEM_LIMIT = 60 * 2**20
MESH = pl.DeviceIdType.MESH

primal_step = 0.5

daubechies_table = [
    [0.7071067811865476, 0.7071067811865476],
    [0.48296291314469025, 0.836516303737469, 0.22414386804185735, -0.12940952255092145],
    [
        0.3326705529509569,
        0.8068915093133388,
        0.4598775021193313,
        -0.13501102001039084,
        -0.08544127388224149,
        0.035226291882100656,
    ],
    [
        0.23037781330885523,
        0.7148465705525415,
        0.6308807679295904,
        -0.02798376941698385,
        -0.18703481171888114,
        0.030841381835986965,
        0.032883011666982945,
        -0.010597401784997278,
    ],
    [
        0.160102397974125,
        0.6038292697974729,
        0.7243085284385744,
        0.13842814590110342,
        -0.24229488706619015,
        -0.03224486958502952,
        0.07757149384006515,
        -0.006241490213011705,
        -0.012580751999015526,
        0.003335725285001549,
    ],
    [
        0.11154074335008017,
        0.4946238903983854,
        0.7511339080215775,
        0.3152503517092432,
        -0.22626469396516913,
        -0.12976686756709563,
        0.09750160558707936,
        0.02752286553001629,
        -0.031582039318031156,
        0.0005538422009938016,
        0.004777257511010651,
        -0.00107730108499558,
    ],
    [
        0.07785205408506236,
        0.39653931948230575,
        0.7291320908465551,
        0.4697822874053586,
        -0.14390600392910627,
        -0.22403618499416572,
        0.07130921926705004,
        0.0806126091510659,
        -0.03802993693503463,
        -0.01657454163101562,
        0.012550998556013784,
        0.00042957797300470274,
        -0.0018016407039998328,
        0.0003537138000010399,
    ],
    [
        0.05441584224308161,
        0.3128715909144659,
        0.6756307362980128,
        0.5853546836548691,
        -0.015829105256023893,
        -0.2840155429624281,
        0.00047248457399797254,
        0.128747426620186,
        -0.01736930100202211,
        -0.04408825393106472,
        0.013981027917015516,
        0.008746094047015655,
        -0.00487035299301066,
        -0.0003917403729959771,
        0.0006754494059985568,
        -0.00011747678400228192,
    ],
]


def tap_pairs(basis):
    taps = np.array(daubechies_table[basis])
    low = taps / np.sum(taps)
    high = np.array([(-1.0) ** t * low[len(low) - 1 - t] for t in range(len(low))])
    return low, high


def composite(basis):
    low, high = tap_pairs(basis)
    n = len(low) // 2
    fine = [{t - n: f[t] for t in range(2 * n)} for f in (low, high)]
    both = []
    for f in (low, high):
        out = {}
        for s in range(2 * n):
            for t in range(2 * n):
                off = (s - n) + 2 * (t - n)
                out[off] = out.get(off, 0.0) + low[s] * f[t]
        both.append(out)
    return fine + both


def halves(matrix):
    high = matrix.astype(np.float32).astype(ml_dtypes.bfloat16)
    low = (matrix - high.astype(np.float64)).astype(np.float32).astype(ml_dtypes.bfloat16)
    return np.stack([high, low])


@functools.lru_cache(maxsize=None)
def matrices(h, w):
    span = h + 2 * REACH
    scale = 1.0 / math.sqrt(BASES)
    a = np.zeros((BASES, 4 * span, BANDS * h))
    b = np.zeros((BASES, BANDS * h, 2 * span))
    c = np.zeros((BASES, 4 * w, 2 * w))
    kinds = [(1, 0), (0, 1), (1, 1), (3, 2), (2, 3), (3, 3), (2, 2)]
    for basis in range(BASES):
        filters = composite(basis)
        rows = np.zeros((4, h, span))
        for kind in range(4):
            for off, tap in filters[kind].items():
                for j in range(h):
                    rows[kind, j, j + REACH + off] += scale * tap
                for j in range(w):
                    c[basis, kind * w + j, (j + off) % (2 * w)] += tap
        for band, (row_kind, col_kind) in enumerate(kinds):
            mat = rows[row_kind]
            a[basis, col_kind * span : (col_kind + 1) * span, band * h : (band + 1) * h] = mat.T
            at = col_kind % 2
            b[basis, band * h : (band + 1) * h, at * span : (at + 1) * span] = mat
    return halves(a), halves(b), halves(c)


def split(x):
    high = x.astype(jnp.bfloat16)
    low = (x - high.astype(jnp.float32)).astype(jnp.bfloat16)
    return high, low


def left_dot(m_high, m_low, x):
    width = x.shape[1]
    high, low = split(x)
    pair = jnp.dot(
        m_high, jnp.concatenate([high, low], axis=1), preferred_element_type=jnp.float32
    )
    rest = jnp.dot(m_low, high, preferred_element_type=jnp.float32)
    return pair[:, :width] + (pair[:, width:] + rest)


def synth_one(x_ref, a_ref, c_ref, k, h, w):
    span = h + 2 * REACH
    z = left_dot(a_ref[0, k], a_ref[1, k], x_ref[k])
    z = jnp.concatenate([z[i * span : (i + 1) * span] for i in range(4)], axis=1)
    high, low = split(z)
    pair = jnp.dot(
        jnp.concatenate([high, low], axis=0), c_ref[0, k], preferred_element_type=jnp.float32
    )
    rest = jnp.dot(high, c_ref[1, k], preferred_element_type=jnp.float32)
    return pair[:span] + (pair[span:] + rest)


def partners():
    return [(dr, dc) for dr in (-2, -1, 0, 1, 2) for dc in (-1, 0, 1) if (dr, dc) != (0, 0)]


def near():
    return [(dr, dc) for dr in (-1, 0, 1) for dc in (-1, 0, 1) if (dr, dc) != (0, 0)]


def overlap(dr, h):
    span = h + 2 * REACH
    shift = h * abs(dr)
    return (shift, 0, span - shift) if dr > 0 else (0, shift, span - shift)


def border(dr, h):
    if dr == 0:
        return (REACH, REACH, h)
    return (h, 0, REACH) if dr > 0 else (REACH, h + REACH, REACH)


def primal_kernel(
    it_ref, gr_ref, x_ref, a_ref, c_ref, e_ref, img_ref,
    acc, held, slots, side, sides_in, bar_sent, bar_recv, send, recv,
):
    h, w = it_ref.shape
    span = h + 2 * REACH
    step = pl.program_id(0)
    nrow, ncol = lax.axis_size("row"), lax.axis_size("col")
    row, col = lax.axis_index("row"), lax.axis_index("col")

    def device(dr, dc):
        return (lax.rem(row + dr + 2 * nrow, nrow), lax.rem(col + dc + ncol, ncol))

    def held_copy(i, dr, dc):
        here, there, rows = border(dr, h)
        return pltpu.make_async_remote_copy(
            src_ref=held.at[1, pl.ds(here, rows)],
            dst_ref=held.at[1 + dc if dc else 3, pl.ds(there, rows)],
            send_sem=bar_sent.at[i], recv_sem=bar_recv.at[i],
            device_id=device(dr, dc), device_id_type=MESH,
        )

    def sum_copy(i, dr, dc):
        here, there, rows = overlap(dr, h)
        slot = dr + 2
        if dc == 0:
            src = acc.at[pl.ds(here, rows)]
            dst = slots.at[slot, pl.ds(there, rows)]
        else:
            src = side.at[(dc + 1) // 2, pl.ds(here, rows)]
            dst = sides_in.at[(dc + 1) // 2, slot, pl.ds(there, rows)]
        return pltpu.make_async_remote_copy(
            src_ref=src, dst_ref=dst, send_sem=send.at[i], recv_sem=recv.at[i],
            device_id=device(dr, dc), device_id_type=MESH,
        )

    @pl.when(step == 0)
    def _():
        barrier = pltpu.get_barrier_semaphore()
        for dr, dc in partners():
            pl.semaphore_signal(barrier, inc=1, device_id=device(dr, dc), device_id_type=MESH)
        held[1, REACH : REACH + h] = it_ref[...]
        acc[...] = jnp.zeros_like(acc)
        acc[REACH : REACH + h, :w] = it_ref[...] - primal_step * gr_ref[...]

    @pl.when(step == 1)
    def _():
        pl.semaphore_wait(pltpu.get_barrier_semaphore(), len(partners()))
        for i, (dr, dc) in enumerate(near()):
            held_copy(i, dr, dc).start()

    total = synth_one(x_ref, a_ref, c_ref, 0, h, w)
    for k in range(1, GROUP):
        total = total + synth_one(x_ref, a_ref, c_ref, k, h, w)
    acc[...] += -primal_step * total

    @pl.when(step == BASES // GROUP - 1)
    def _():
        left = lax.broadcasted_iota(jnp.int32, (span, w), 1) < w // 2
        mine, over = acc[:, :w], acc[:, w:]
        side[0] = jnp.where(left, mine, over)
        side[1] = jnp.where(left, over, mine)
        for i, (dr, dc) in enumerate(partners()):
            sum_copy(i, dr, dc).start()
        for i, (dr, dc) in enumerate(near()):
            held_copy(i, dr, dc).wait()
        for i, (dr, dc) in enumerate(partners()):
            sum_copy(i, dr, dc).wait()

        def gather(read, start):
            total = start
            for dr in (-2, -1, 0, 1, 2):
                if dr == 0 and start is not None:
                    continue
                _, there, rows = overlap(dr, h)
                part = read(dr + 2, there, rows)
                sizes = (there, span - there - rows)
                above, below = [jnp.zeros((n, part.shape[1]), jnp.float32) for n in sizes]
                blocks = [above] * (there > 0) + [part] + [below] * (sizes[1] > 0)
                part = jnp.concatenate(blocks, axis=0) if len(blocks) > 1 else part
                total = part if total is None else total + part
            return total

        mid = gather(lambda s, t, n: slots[s, t : t + n], acc[...])
        from_right = gather(lambda s, t, n: sides_in[0, s, t : t + n], None)
        from_left = gather(lambda s, t, n: sides_in[1, s, t : t + n], None)
        inner = mid[:, :w] + jnp.where(left, from_left, from_right)
        outer = mid[:, w:] + jnp.where(left, from_right, from_left)
        inner = jnp.maximum(inner, 0.0)
        outer = jnp.maximum(outer, 0.0)
        img_ref[...] = inner[REACH : REACH + h]
        it_inner = jnp.concatenate(
            [held[3, :REACH], held[1, REACH : REACH + h], held[3, REACH + h :]], axis=0
        )
        it_outer = jnp.where(left, held[0], held[2])
        ext = jnp.concatenate([2.0 * inner - it_inner, 2.0 * outer - it_outer], axis=1)
        high, low = split(ext)
        e_ref[:span] = high
        e_ref[span:] = low


def dual_kernel(wt_ref, e_ref, img_ref, x_ref, b_ref, c_ref, img_out, x_out):
    h, w = img_ref.shape
    span = h + 2 * REACH
    step = pl.program_id(0)

    @pl.when(step == 0)
    def _():
        img_out[...] = img_ref[...]

    across = (((1,), (1,)), ((), ()))
    for k in range(GROUP):
        pair = lax.dot_general(
            e_ref[...], c_ref[0, k], across, preferred_element_type=jnp.float32
        )
        rest = lax.dot_general(
            e_ref[:span], c_ref[1, k], across, preferred_element_type=jnp.float32
        )
        z = pair[:span] + (pair[span:] + rest)
        for first, last, at in ((0, 3, 0), (3, 7, 2)):
            data = jnp.concatenate(
                [z[:, at * w : (at + 1) * w], z[:, (at + 1) * w : (at + 2) * w]], axis=0
            )
            rows = slice(first * h, last * h)
            coeffs = left_dot(b_ref[0, k, rows], b_ref[1, k, rows], data)
            for band in range(first, last):
                bound = wt_ref[step * GROUP + k, band]
                value = x_ref[k, band * h : (band + 1) * h]
                value = value + coeffs[(band - first) * h : (band - first + 1) * h]
                x_out[k, band * h : (band + 1) * h] = jnp.clip(value, -bound, bound)


def on_device(iterate, gradient, dual_coeffs, weights):
    h, w = iterate.shape
    span = h + 2 * REACH
    a, b, c = [jnp.asarray(m) for m in matrices(h, w)]
    duals = dual_coeffs.reshape(BASES, BANDS * h, w)
    whole = pl.BlockSpec((h, w), lambda i: (0, 0))
    per_basis = pl.BlockSpec((GROUP, BANDS * h, w), lambda i: (i, 0, 0))
    halved = lambda m: pl.BlockSpec((2, GROUP) + m.shape[2:], lambda i: (0, i, 0, 0))
    ext, image = pl.pallas_call(
        primal_kernel,
        grid=(BASES // GROUP,),
        out_shape=(
            jax.ShapeDtypeStruct((2 * span, 2 * w), jnp.bfloat16),
            jax.ShapeDtypeStruct((h, w), jnp.float32),
        ),
        in_specs=[whole, whole, per_basis, halved(a), halved(c)],
        out_specs=(pl.BlockSpec((2 * span, 2 * w), lambda i: (0, 0)), whole),
        scratch_shapes=[
            pltpu.VMEM((span, 2 * w), jnp.float32),
            pltpu.VMEM((4, span, w), jnp.float32),
            pltpu.VMEM((5, span, 2 * w), jnp.float32),
            pltpu.VMEM((2, span, w), jnp.float32),
            pltpu.VMEM((2, 5, span, w), jnp.float32),
            pltpu.SemaphoreType.DMA((8,)),
            pltpu.SemaphoreType.DMA((8,)),
            pltpu.SemaphoreType.DMA((14,)),
            pltpu.SemaphoreType.DMA((14,)),
        ],
        compiler_params=pltpu.CompilerParams(
            collective_id=0, has_side_effects=True, vmem_limit_bytes=VMEM_LIMIT
        ),
    )(iterate, gradient, duals, a, c)
    new_image, new_duals = pl.pallas_call(
        dual_kernel,
        grid=(BASES // GROUP,),
        out_shape=(
            jax.ShapeDtypeStruct((h, w), jnp.float32),
            jax.ShapeDtypeStruct(duals.shape, jnp.float32),
        ),
        in_specs=[
            pl.BlockSpec(memory_space=pltpu.SMEM),
            pl.BlockSpec((2 * span, 2 * w), lambda i: (0, 0)),
            whole,
            per_basis,
            halved(b),
            halved(c),
        ],
        out_specs=(whole, per_basis),
        compiler_params=pltpu.CompilerParams(vmem_limit_bytes=VMEM_LIMIT),
    )(weights, ext, image, duals, b, c)
    return new_image, new_duals.reshape(dual_coeffs.shape)


def solution(mesh):
    return jax.shard_map(
        on_device,
        mesh=mesh,
        in_specs=(P("row", "col"), P("row", "col"), P(None, None, "row", "col"), P()),
        out_specs=(P("row", "col"), P(None, None, "row", "col")),
        check_vma=False,
    )
```

```python
import functools
import math

import jax
import jax.numpy as jnp
import ml_dtypes
import numpy as np
from jax import lax
from jax.experimental import pallas as pl
from jax.experimental.pallas import tpu as pltpu
from jax.sharding import PartitionSpec as P

BASES = 8
BANDS = 7
REACH = 24
GROUP = 2
VMEM_LIMIT = 60 * 2**20
MESH = pl.DeviceIdType.MESH

primal_step = 0.5

daubechies_table = [
    [0.7071067811865476, 0.7071067811865476],
    [0.48296291314469025, 0.836516303737469, 0.22414386804185735, -0.12940952255092145],
    [
        0.3326705529509569,
        0.8068915093133388,
        0.4598775021193313,
        -0.13501102001039084,
        -0.08544127388224149,
        0.035226291882100656,
    ],
    [
        0.23037781330885523,
        0.7148465705525415,
        0.6308807679295904,
        -0.02798376941698385,
        -0.18703481171888114,
        0.030841381835986965,
        0.032883011666982945,
        -0.010597401784997278,
    ],
    [
        0.160102397974125,
        0.6038292697974729,
        0.7243085284385744,
        0.13842814590110342,
        -0.24229488706619015,
        -0.03224486958502952,
        0.07757149384006515,
        -0.006241490213011705,
        -0.012580751999015526,
        0.003335725285001549,
    ],
    [
        0.11154074335008017,
        0.4946238903983854,
        0.7511339080215775,
        0.3152503517092432,
        -0.22626469396516913,
        -0.12976686756709563,
        0.09750160558707936,
        0.02752286553001629,
        -0.031582039318031156,
        0.0005538422009938016,
        0.004777257511010651,
        -0.00107730108499558,
    ],
    [
        0.07785205408506236,
        0.39653931948230575,
        0.7291320908465551,
        0.4697822874053586,
        -0.14390600392910627,
        -0.22403618499416572,
        0.07130921926705004,
        0.0806126091510659,
        -0.03802993693503463,
        -0.01657454163101562,
        0.012550998556013784,
        0.00042957797300470274,
        -0.0018016407039998328,
        0.0003537138000010399,
    ],
    [
        0.05441584224308161,
        0.3128715909144659,
        0.6756307362980128,
        0.5853546836548691,
        -0.015829105256023893,
        -0.2840155429624281,
        0.00047248457399797254,
        0.128747426620186,
        -0.01736930100202211,
        -0.04408825393106472,
        0.013981027917015516,
        0.008746094047015655,
        -0.00487035299301066,
        -0.0003917403729959771,
        0.0006754494059985568,
        -0.00011747678400228192,
    ],
]


def tap_pairs(basis):
    taps = np.array(daubechies_table[basis])
    low = taps / np.sum(taps)
    high = np.array([(-1.0) ** t * low[len(low) - 1 - t] for t in range(len(low))])
    return low, high


def composite(basis):
    low, high = tap_pairs(basis)
    n = len(low) // 2
    fine = [{t - n: f[t] for t in range(2 * n)} for f in (low, high)]
    both = []
    for f in (low, high):
        out = {}
        for s in range(2 * n):
            for t in range(2 * n):
                off = (s - n) + 2 * (t - n)
                out[off] = out.get(off, 0.0) + low[s] * f[t]
        both.append(out)
    return fine + both


def halves(matrix):
    high = matrix.astype(np.float32).astype(ml_dtypes.bfloat16)
    low = (matrix - high.astype(np.float64)).astype(np.float32).astype(ml_dtypes.bfloat16)
    return np.stack([high, low])


@functools.lru_cache(maxsize=None)
def matrices(h, w):
    span = h + 2 * REACH
    scale = 1.0 / math.sqrt(BASES)
    a = np.zeros((BASES, 4 * span, BANDS * h))
    b = np.zeros((BASES, BANDS * h, 2 * span))
    c = np.zeros((BASES, 8, 2 * w), np.float32)
    kinds = [(1, 0), (0, 1), (1, 1), (3, 2), (2, 3), (3, 3), (2, 2)]
    for basis in range(BASES):
        filters = composite(basis)
        rows = np.zeros((4, h, span))
        for kind in range(4):
            for off, tap in filters[kind].items():
                for j in range(h):
                    rows[kind, j, j + REACH + off] += scale * tap
                c[basis, kind, off % (2 * w)] += tap
        for band, (row_kind, col_kind) in enumerate(kinds):
            mat = rows[row_kind]
            a[basis, col_kind * span : (col_kind + 1) * span, band * h : (band + 1) * h] = mat.T
            at = col_kind % 2
            b[basis, band * h : (band + 1) * h, at * span : (at + 1) * span] = mat
    return halves(a), halves(b), c


def split(x):
    high = x.astype(jnp.bfloat16)
    low = (x - high.astype(jnp.float32)).astype(jnp.bfloat16)
    return high, low


def column_matrix(c_ref, k, w):
    parts = []
    for kind in range(4):
        first = jnp.broadcast_to(c_ref[k, kind : kind + 1], (w, 2 * w))
        parts.append(pltpu.roll(first, 0, 1, stride=1, stride_axis=0))
    return split(jnp.concatenate(parts, axis=0))


def left_dot(m_high, m_low, x):
    width = x.shape[1]
    high, low = split(x)
    pair = jnp.dot(
        m_high, jnp.concatenate([high, low], axis=1), preferred_element_type=jnp.float32
    )
    rest = jnp.dot(m_low, high, preferred_element_type=jnp.float32)
    return pair[:, :width] + (pair[:, width:] + rest)


def synth_one(x_ref, a_ref, c_ref, k, h, w):
    span = h + 2 * REACH
    z = left_dot(a_ref[0, k], a_ref[1, k], x_ref[k])
    z = jnp.concatenate([z[i * span : (i + 1) * span] for i in range(4)], axis=1)
    high, low = split(z)
    c_high, c_low = column_matrix(c_ref, k, w)
    pair = jnp.dot(
        jnp.concatenate([high, low], axis=0), c_high, preferred_element_type=jnp.float32
    )
    rest = jnp.dot(high, c_low, preferred_element_type=jnp.float32)
    return pair[:span] + (pair[span:] + rest)


def partners():
    return [(dr, dc) for dr in (-2, -1, 0, 1, 2) for dc in (-1, 0, 1) if (dr, dc) != (0, 0)]


def near():
    return [(dr, dc) for dr in (-1, 0, 1) for dc in (-1, 0, 1) if (dr, dc) != (0, 0)]


def overlap(dr, h):
    span = h + 2 * REACH
    shift = h * abs(dr)
    return (shift, 0, span - shift) if dr > 0 else (0, shift, span - shift)


def border(dr, h):
    if dr == 0:
        return (REACH, REACH, h)
    return (h, 0, REACH) if dr > 0 else (REACH, h + REACH, REACH)


def primal_kernel(
    it_ref, gr_ref, x_ref, a_ref, c_ref, e_ref, img_ref,
    acc, held, slots, side, sides_in, bar_sent, bar_recv, send, recv,
):
    h, w = it_ref.shape
    span = h + 2 * REACH
    step = pl.program_id(0)
    nrow, ncol = lax.axis_size("row"), lax.axis_size("col")
    row, col = lax.axis_index("row"), lax.axis_index("col")

    def device(dr, dc):
        return (lax.rem(row + dr + 2 * nrow, nrow), lax.rem(col + dc + ncol, ncol))

    def held_copy(i, dr, dc):
        here, there, rows = border(dr, h)
        return pltpu.make_async_remote_copy(
            src_ref=held.at[1, pl.ds(here, rows)],
            dst_ref=held.at[1 + dc if dc else 3, pl.ds(there, rows)],
            send_sem=bar_sent.at[i], recv_sem=bar_recv.at[i],
            device_id=device(dr, dc), device_id_type=MESH,
        )

    def sum_copy(i, dr, dc):
        here, there, rows = overlap(dr, h)
        slot = dr + 2
        if dc == 0:
            src = acc.at[pl.ds(here, rows)]
            dst = slots.at[slot, pl.ds(there, rows)]
        else:
            src = side.at[(dc + 1) // 2, pl.ds(here, rows)]
            dst = sides_in.at[(dc + 1) // 2, slot, pl.ds(there, rows)]
        return pltpu.make_async_remote_copy(
            src_ref=src, dst_ref=dst, send_sem=send.at[i], recv_sem=recv.at[i],
            device_id=device(dr, dc), device_id_type=MESH,
        )

    @pl.when(step == 0)
    def _():
        barrier = pltpu.get_barrier_semaphore()
        for dr, dc in partners():
            pl.semaphore_signal(barrier, inc=1, device_id=device(dr, dc), device_id_type=MESH)
        held[1, REACH : REACH + h] = it_ref[...]
        acc[...] = jnp.zeros_like(acc)
        acc[REACH : REACH + h, :w] = it_ref[...] - primal_step * gr_ref[...]

    @pl.when(step == 1)
    def _():
        pl.semaphore_wait(pltpu.get_barrier_semaphore(), len(partners()))
        for i, (dr, dc) in enumerate(near()):
            held_copy(i, dr, dc).start()

    total = synth_one(x_ref, a_ref, c_ref, 0, h, w)
    for k in range(1, GROUP):
        total = total + synth_one(x_ref, a_ref, c_ref, k, h, w)
    acc[...] += -primal_step * total

    @pl.when(step == BASES // GROUP - 1)
    def _():
        left = lax.broadcasted_iota(jnp.int32, (span, w), 1) < w // 2
        mine, over = acc[:, :w], acc[:, w:]
        side[0] = jnp.where(left, mine, over)
        side[1] = jnp.where(left, over, mine)
        for i, (dr, dc) in enumerate(partners()):
            sum_copy(i, dr, dc).start()
        for i, (dr, dc) in enumerate(near()):
            held_copy(i, dr, dc).wait()
        for i, (dr, dc) in enumerate(partners()):
            sum_copy(i, dr, dc).wait()

        def gather(read, start):
            total = start
            for dr in (-2, -1, 0, 1, 2):
                if dr == 0 and start is not None:
                    continue
                _, there, rows = overlap(dr, h)
                part = read(dr + 2, there, rows)
                sizes = (there, span - there - rows)
                above, below = [jnp.zeros((n, part.shape[1]), jnp.float32) for n in sizes]
                blocks = [above] * (there > 0) + [part] + [below] * (sizes[1] > 0)
                part = jnp.concatenate(blocks, axis=0) if len(blocks) > 1 else part
                total = part if total is None else total + part
            return total

        mid = gather(lambda s, t, n: slots[s, t : t + n], acc[...])
        from_right = gather(lambda s, t, n: sides_in[0, s, t : t + n], None)
        from_left = gather(lambda s, t, n: sides_in[1, s, t : t + n], None)
        inner = mid[:, :w] + jnp.where(left, from_left, from_right)
        outer = mid[:, w:] + jnp.where(left, from_right, from_left)
        inner = jnp.maximum(inner, 0.0)
        outer = jnp.maximum(outer, 0.0)
        img_ref[...] = inner[REACH : REACH + h]
        it_inner = jnp.concatenate(
            [held[3, :REACH], held[1, REACH : REACH + h], held[3, REACH + h :]], axis=0
        )
        it_outer = jnp.where(left, held[0], held[2])
        ext = jnp.concatenate([2.0 * inner - it_inner, 2.0 * outer - it_outer], axis=1)
        high, low = split(ext)
        e_ref[:span] = high
        e_ref[span:] = low


def dual_kernel(wt_ref, e_ref, img_ref, x_ref, b_ref, c_ref, img_out, x_out):
    h, w = img_ref.shape
    span = h + 2 * REACH
    step = pl.program_id(0)

    @pl.when(step == 0)
    def _():
        img_out[...] = img_ref[...]

    across = (((1,), (1,)), ((), ()))
    for k in range(GROUP):
        c_high, c_low = column_matrix(c_ref, k, w)
        pair = lax.dot_general(
            e_ref[...], c_high, across, preferred_element_type=jnp.float32
        )
        rest = lax.dot_general(
            e_ref[:span], c_low, across, preferred_element_type=jnp.float32
        )
        z = pair[:span] + (pair[span:] + rest)
        for first, last, at in ((0, 3, 0), (3, 7, 2)):
            data = jnp.concatenate(
                [z[:, at * w : (at + 1) * w], z[:, (at + 1) * w : (at + 2) * w]], axis=0
            )
            rows = slice(first * h, last * h)
            coeffs = left_dot(b_ref[0, k, rows], b_ref[1, k, rows], data)
            for band in range(first, last):
                bound = wt_ref[step * GROUP + k, band]
                value = x_ref[k, band * h : (band + 1) * h]
                value = value + coeffs[(band - first) * h : (band - first + 1) * h]
                x_out[k, band * h : (band + 1) * h] = jnp.clip(value, -bound, bound)


def on_device(iterate, gradient, dual_coeffs, weights):
    h, w = iterate.shape
    span = h + 2 * REACH
    a, b, c = [jnp.asarray(m) for m in matrices(h, w)]
    duals = dual_coeffs.reshape(BASES, BANDS * h, w)
    whole = pl.BlockSpec((h, w), lambda i: (0, 0))
    per_basis = pl.BlockSpec((GROUP, BANDS * h, w), lambda i: (i, 0, 0))
    first_rows = pl.BlockSpec((GROUP, 8, 2 * w), lambda i: (i, 0, 0))
    halved = lambda m: pl.BlockSpec((2, GROUP) + m.shape[2:], lambda i: (0, i, 0, 0))
    ext, image = pl.pallas_call(
        primal_kernel,
        grid=(BASES // GROUP,),
        out_shape=(
            jax.ShapeDtypeStruct((2 * span, 2 * w), jnp.bfloat16),
            jax.ShapeDtypeStruct((h, w), jnp.float32),
        ),
        in_specs=[whole, whole, per_basis, halved(a), first_rows],
        out_specs=(pl.BlockSpec((2 * span, 2 * w), lambda i: (0, 0)), whole),
        scratch_shapes=[
            pltpu.VMEM((span, 2 * w), jnp.float32),
            pltpu.VMEM((4, span, w), jnp.float32),
            pltpu.VMEM((5, span, 2 * w), jnp.float32),
            pltpu.VMEM((2, span, w), jnp.float32),
            pltpu.VMEM((2, 5, span, w), jnp.float32),
            pltpu.SemaphoreType.DMA((8,)),
            pltpu.SemaphoreType.DMA((8,)),
            pltpu.SemaphoreType.DMA((14,)),
            pltpu.SemaphoreType.DMA((14,)),
        ],
        compiler_params=pltpu.CompilerParams(
            collective_id=0, has_side_effects=True, vmem_limit_bytes=VMEM_LIMIT
        ),
    )(iterate, gradient, duals, a, c)
    new_image, new_duals = pl.pallas_call(
        dual_kernel,
        grid=(BASES // GROUP,),
        out_shape=(
            jax.ShapeDtypeStruct((h, w), jnp.float32),
            jax.ShapeDtypeStruct(duals.shape, jnp.float32),
        ),
        in_specs=[
            pl.BlockSpec(memory_space=pltpu.SMEM),
            pl.BlockSpec((2 * span, 2 * w), lambda i: (0, 0)),
            whole,
            per_basis,
            halved(b),
            first_rows,
        ],
        out_specs=(whole, per_basis),
        compiler_params=pltpu.CompilerParams(vmem_limit_bytes=VMEM_LIMIT),
    )(weights, ext, image, duals, b, c)
    return new_image, new_duals.reshape(dual_coeffs.shape)


def solution(mesh):
    return jax.shard_map(
        on_device,
        mesh=mesh,
        in_specs=(P("row", "col"), P("row", "col"), P(None, None, "row", "col"), P()),
        out_specs=(P("row", "col"), P(None, None, "row", "col")),
        check_vma=False,
    )
```

```python
import functools
import math

import jax
import jax.numpy as jnp
import ml_dtypes
import numpy as np
from jax import lax
from jax.experimental import pallas as pl
from jax.experimental.pallas import tpu as pltpu
from jax.sharding import PartitionSpec as P

BASES = 8
BANDS = 7
REACH = 24
GROUP = 4
VMEM_LIMIT = 60 * 2**20
MESH = pl.DeviceIdType.MESH

primal_step = 0.5

daubechies_table = [
    [0.7071067811865476, 0.7071067811865476],
    [0.48296291314469025, 0.836516303737469, 0.22414386804185735, -0.12940952255092145],
    [
        0.3326705529509569,
        0.8068915093133388,
        0.4598775021193313,
        -0.13501102001039084,
        -0.08544127388224149,
        0.035226291882100656,
    ],
    [
        0.23037781330885523,
        0.7148465705525415,
        0.6308807679295904,
        -0.02798376941698385,
        -0.18703481171888114,
        0.030841381835986965,
        0.032883011666982945,
        -0.010597401784997278,
    ],
    [
        0.160102397974125,
        0.6038292697974729,
        0.7243085284385744,
        0.13842814590110342,
        -0.24229488706619015,
        -0.03224486958502952,
        0.07757149384006515,
        -0.006241490213011705,
        -0.012580751999015526,
        0.003335725285001549,
    ],
    [
        0.11154074335008017,
        0.4946238903983854,
        0.7511339080215775,
        0.3152503517092432,
        -0.22626469396516913,
        -0.12976686756709563,
        0.09750160558707936,
        0.02752286553001629,
        -0.031582039318031156,
        0.0005538422009938016,
        0.004777257511010651,
        -0.00107730108499558,
    ],
    [
        0.07785205408506236,
        0.39653931948230575,
        0.7291320908465551,
        0.4697822874053586,
        -0.14390600392910627,
        -0.22403618499416572,
        0.07130921926705004,
        0.0806126091510659,
        -0.03802993693503463,
        -0.01657454163101562,
        0.012550998556013784,
        0.00042957797300470274,
        -0.0018016407039998328,
        0.0003537138000010399,
    ],
    [
        0.05441584224308161,
        0.3128715909144659,
        0.6756307362980128,
        0.5853546836548691,
        -0.015829105256023893,
        -0.2840155429624281,
        0.00047248457399797254,
        0.128747426620186,
        -0.01736930100202211,
        -0.04408825393106472,
        0.013981027917015516,
        0.008746094047015655,
        -0.00487035299301066,
        -0.0003917403729959771,
        0.0006754494059985568,
        -0.00011747678400228192,
    ],
]


def tap_pairs(basis):
    taps = np.array(daubechies_table[basis])
    low = taps / np.sum(taps)
    high = np.array([(-1.0) ** t * low[len(low) - 1 - t] for t in range(len(low))])
    return low, high


def composite(basis):
    low, high = tap_pairs(basis)
    n = len(low) // 2
    fine = [{t - n: f[t] for t in range(2 * n)} for f in (low, high)]
    both = []
    for f in (low, high):
        out = {}
        for s in range(2 * n):
            for t in range(2 * n):
                off = (s - n) + 2 * (t - n)
                out[off] = out.get(off, 0.0) + low[s] * f[t]
        both.append(out)
    return fine + both


def halves(matrix):
    high = matrix.astype(np.float32).astype(ml_dtypes.bfloat16)
    low = (matrix - high.astype(np.float64)).astype(np.float32).astype(ml_dtypes.bfloat16)
    return np.stack([high, low])


@functools.lru_cache(maxsize=None)
def matrices(h, w):
    span = h + 2 * REACH
    scale = 1.0 / math.sqrt(BASES)
    a = np.zeros((BASES, 4 * span, BANDS * h))
    b = np.zeros((BASES, BANDS * h, 2 * span))
    c = np.zeros((BASES, 8, 2 * w), np.float32)
    kinds = [(1, 0), (0, 1), (1, 1), (3, 2), (2, 3), (3, 3), (2, 2)]
    for basis in range(BASES):
        filters = composite(basis)
        rows = np.zeros((4, h, span))
        for kind in range(4):
            for off, tap in filters[kind].items():
                for j in range(h):
                    rows[kind, j, j + REACH + off] += scale * tap
                c[basis, kind, off % (2 * w)] += tap
        for band, (row_kind, col_kind) in enumerate(kinds):
            mat = rows[row_kind]
            a[basis, col_kind * span : (col_kind + 1) * span, band * h : (band + 1) * h] = mat.T
            at = col_kind % 2
            b[basis, band * h : (band + 1) * h, at * span : (at + 1) * span] = mat
    return halves(a), halves(b), c


def split(x):
    high = x.astype(jnp.bfloat16)
    low = (x - high.astype(jnp.float32)).astype(jnp.bfloat16)
    return high, low


def column_matrix(c_ref, k, w):
    parts = []
    for kind in range(4):
        first = jnp.broadcast_to(c_ref[k, kind : kind + 1], (w, 2 * w))
        parts.append(pltpu.roll(first, 0, 1, stride=1, stride_axis=0))
    return split(jnp.concatenate(parts, axis=0))


def left_dot(m_high, m_low, x):
    width = x.shape[1]
    high, low = split(x)
    pair = jnp.dot(
        m_high, jnp.concatenate([high, low], axis=1), preferred_element_type=jnp.float32
    )
    rest = jnp.dot(m_low, high, preferred_element_type=jnp.float32)
    return pair[:, :width] + (pair[:, width:] + rest)


def synth_one(x_ref, a_ref, c_ref, k, h, w):
    span = h + 2 * REACH
    z = left_dot(a_ref[0, k], a_ref[1, k], x_ref[k])
    z = jnp.concatenate([z[i * span : (i + 1) * span] for i in range(4)], axis=1)
    high, low = split(z)
    c_high, c_low = column_matrix(c_ref, k, w)
    pair = jnp.dot(
        jnp.concatenate([high, low], axis=0), c_high, preferred_element_type=jnp.float32
    )
    rest = jnp.dot(high, c_low, preferred_element_type=jnp.float32)
    return pair[:span] + (pair[span:] + rest)


def partners():
    return [(dr, dc) for dr in (-2, -1, 0, 1, 2) for dc in (-1, 0, 1) if (dr, dc) != (0, 0)]


def near():
    return [(dr, dc) for dr in (-1, 0, 1) for dc in (-1, 0, 1) if (dr, dc) != (0, 0)]


def overlap(dr, h):
    span = h + 2 * REACH
    shift = h * abs(dr)
    return (shift, 0, span - shift) if dr > 0 else (0, shift, span - shift)


def border(dr, h):
    if dr == 0:
        return (REACH, REACH, h)
    return (h, 0, REACH) if dr > 0 else (REACH, h + REACH, REACH)


def primal_kernel(
    it_ref, gr_ref, x_ref, a_ref, c_ref, e_ref, img_ref,
    acc, held, slots, side, sides_in, bar_sent, bar_recv, send, recv,
):
    h, w = it_ref.shape
    span = h + 2 * REACH
    step = pl.program_id(0)
    nrow, ncol = lax.axis_size("row"), lax.axis_size("col")
    row, col = lax.axis_index("row"), lax.axis_index("col")

    def device(dr, dc):
        return (lax.rem(row + dr + 2 * nrow, nrow), lax.rem(col + dc + ncol, ncol))

    def held_copy(i, dr, dc):
        here, there, rows = border(dr, h)
        return pltpu.make_async_remote_copy(
            src_ref=held.at[1, pl.ds(here, rows)],
            dst_ref=held.at[1 + dc if dc else 3, pl.ds(there, rows)],
            send_sem=bar_sent.at[i], recv_sem=bar_recv.at[i],
            device_id=device(dr, dc), device_id_type=MESH,
        )

    def sum_copy(i, dr, dc):
        here, there, rows = overlap(dr, h)
        slot = dr + 2
        if dc == 0:
            src = acc.at[pl.ds(here, rows)]
            dst = slots.at[slot, pl.ds(there, rows)]
        else:
            src = side.at[(dc + 1) // 2, pl.ds(here, rows)]
            dst = sides_in.at[(dc + 1) // 2, slot, pl.ds(there, rows)]
        return pltpu.make_async_remote_copy(
            src_ref=src, dst_ref=dst, send_sem=send.at[i], recv_sem=recv.at[i],
            device_id=device(dr, dc), device_id_type=MESH,
        )

    @pl.when(step == 0)
    def _():
        barrier = pltpu.get_barrier_semaphore()
        for dr, dc in partners():
            pl.semaphore_signal(barrier, inc=1, device_id=device(dr, dc), device_id_type=MESH)
        held[1, REACH : REACH + h] = it_ref[...]
        acc[...] = jnp.zeros_like(acc)
        acc[REACH : REACH + h, :w] = it_ref[...] - primal_step * gr_ref[...]

    @pl.when(step == 1)
    def _():
        pl.semaphore_wait(pltpu.get_barrier_semaphore(), len(partners()))
        for i, (dr, dc) in enumerate(near()):
            held_copy(i, dr, dc).start()

    total = synth_one(x_ref, a_ref, c_ref, 0, h, w)
    for k in range(1, GROUP):
        total = total + synth_one(x_ref, a_ref, c_ref, k, h, w)
    acc[...] += -primal_step * total

    @pl.when(step == BASES // GROUP - 1)
    def _():
        left = lax.broadcasted_iota(jnp.int32, (span, w), 1) < w // 2
        mine, over = acc[:, :w], acc[:, w:]
        side[0] = jnp.where(left, mine, over)
        side[1] = jnp.where(left, over, mine)
        for i, (dr, dc) in enumerate(partners()):
            sum_copy(i, dr, dc).start()
        for i, (dr, dc) in enumerate(near()):
            held_copy(i, dr, dc).wait()
        for i, (dr, dc) in enumerate(partners()):
            sum_copy(i, dr, dc).wait()

        def gather(read, start):
            total = start
            for dr in (-2, -1, 0, 1, 2):
                if dr == 0 and start is not None:
                    continue
                _, there, rows = overlap(dr, h)
                part = read(dr + 2, there, rows)
                sizes = (there, span - there - rows)
                above, below = [jnp.zeros((n, part.shape[1]), jnp.float32) for n in sizes]
                blocks = [above] * (there > 0) + [part] + [below] * (sizes[1] > 0)
                part = jnp.concatenate(blocks, axis=0) if len(blocks) > 1 else part
                total = part if total is None else total + part
            return total

        mid = gather(lambda s, t, n: slots[s, t : t + n], acc[...])
        from_right = gather(lambda s, t, n: sides_in[0, s, t : t + n], None)
        from_left = gather(lambda s, t, n: sides_in[1, s, t : t + n], None)
        inner = mid[:, :w] + jnp.where(left, from_left, from_right)
        outer = mid[:, w:] + jnp.where(left, from_right, from_left)
        inner = jnp.maximum(inner, 0.0)
        outer = jnp.maximum(outer, 0.0)
        img_ref[...] = inner[REACH : REACH + h]
        it_inner = jnp.concatenate(
            [held[3, :REACH], held[1, REACH : REACH + h], held[3, REACH + h :]], axis=0
        )
        it_outer = jnp.where(left, held[0], held[2])
        ext = jnp.concatenate([2.0 * inner - it_inner, 2.0 * outer - it_outer], axis=1)
        high, low = split(ext)
        e_ref[:span] = high
        e_ref[span:] = low


def dual_kernel(wt_ref, e_ref, img_ref, x_ref, b_ref, c_ref, img_out, x_out):
    h, w = img_ref.shape
    span = h + 2 * REACH
    step = pl.program_id(0)

    @pl.when(step == 0)
    def _():
        img_out[...] = img_ref[...]

    across = (((1,), (1,)), ((), ()))
    for k in range(GROUP):
        c_high, c_low = column_matrix(c_ref, k, w)
        pair = lax.dot_general(
            e_ref[...], c_high, across, preferred_element_type=jnp.float32
        )
        rest = lax.dot_general(
            e_ref[:span], c_low, across, preferred_element_type=jnp.float32
        )
        z = pair[:span] + (pair[span:] + rest)
        for first, last, at in ((0, 3, 0), (3, 7, 2)):
            data = jnp.concatenate(
                [z[:, at * w : (at + 1) * w], z[:, (at + 1) * w : (at + 2) * w]], axis=0
            )
            rows = slice(first * h, last * h)
            coeffs = left_dot(b_ref[0, k, rows], b_ref[1, k, rows], data)
            for band in range(first, last):
                bound = wt_ref[step * GROUP + k, band]
                value = x_ref[k, band * h : (band + 1) * h]
                value = value + coeffs[(band - first) * h : (band - first + 1) * h]
                x_out[k, band * h : (band + 1) * h] = jnp.clip(value, -bound, bound)


def on_device(iterate, gradient, dual_coeffs, weights):
    h, w = iterate.shape
    span = h + 2 * REACH
    a, b, c = [jnp.asarray(m) for m in matrices(h, w)]
    duals = dual_coeffs.reshape(BASES, BANDS * h, w)
    whole = pl.BlockSpec((h, w), lambda i: (0, 0))
    per_basis = pl.BlockSpec((GROUP, BANDS * h, w), lambda i: (i, 0, 0))
    first_rows = pl.BlockSpec((GROUP, 8, 2 * w), lambda i: (i, 0, 0))
    halved = lambda m: pl.BlockSpec((2, GROUP) + m.shape[2:], lambda i: (0, i, 0, 0))
    ext, image = pl.pallas_call(
        primal_kernel,
        grid=(BASES // GROUP,),
        out_shape=(
            jax.ShapeDtypeStruct((2 * span, 2 * w), jnp.bfloat16),
            jax.ShapeDtypeStruct((h, w), jnp.float32),
        ),
        in_specs=[whole, whole, per_basis, halved(a), first_rows],
        out_specs=(pl.BlockSpec((2 * span, 2 * w), lambda i: (0, 0)), whole),
        scratch_shapes=[
            pltpu.VMEM((span, 2 * w), jnp.float32),
            pltpu.VMEM((4, span, w), jnp.float32),
            pltpu.VMEM((5, span, 2 * w), jnp.float32),
            pltpu.VMEM((2, span, w), jnp.float32),
            pltpu.VMEM((2, 5, span, w), jnp.float32),
            pltpu.SemaphoreType.DMA((8,)),
            pltpu.SemaphoreType.DMA((8,)),
            pltpu.SemaphoreType.DMA((14,)),
            pltpu.SemaphoreType.DMA((14,)),
        ],
        compiler_params=pltpu.CompilerParams(
            collective_id=0, has_side_effects=True, vmem_limit_bytes=VMEM_LIMIT
        ),
    )(iterate, gradient, duals, a, c)
    new_image, new_duals = pl.pallas_call(
        dual_kernel,
        grid=(BASES // GROUP,),
        out_shape=(
            jax.ShapeDtypeStruct((h, w), jnp.float32),
            jax.ShapeDtypeStruct(duals.shape, jnp.float32),
        ),
        in_specs=[
            pl.BlockSpec(memory_space=pltpu.SMEM),
            pl.BlockSpec((2 * span, 2 * w), lambda i: (0, 0)),
            whole,
            per_basis,
            halved(b),
            first_rows,
        ],
        out_specs=(whole, per_basis),
        compiler_params=pltpu.CompilerParams(vmem_limit_bytes=VMEM_LIMIT),
    )(weights, ext, image, duals, b, c)
    return new_image, new_duals.reshape(dual_coeffs.shape)


def solution(mesh):
    return jax.shard_map(
        on_device,
        mesh=mesh,
        in_specs=(P("row", "col"), P("row", "col"), P(None, None, "row", "col"), P()),
        out_specs=(P("row", "col"), P(None, None, "row", "col")),
        check_vma=False,
    )
```

```python
import functools
import math

import jax
import jax.numpy as jnp
import ml_dtypes
import numpy as np
from jax import lax
from jax.experimental import pallas as pl
from jax.experimental.pallas import tpu as pltpu
from jax.sharding import PartitionSpec as P

BASES = 8
BANDS = 7
REACH = 24
GROUP = 4
VMEM_LIMIT = 60 * 2**20
COLUMN_BANDS = [(0,), (1, 2), (3, 6), (4, 5)]
BAND_ORDER = [0, 1, 2, 3, 6, 4, 5]
MESH = pl.DeviceIdType.MESH

primal_step = 0.5

daubechies_table = [
    [0.7071067811865476, 0.7071067811865476],
    [0.48296291314469025, 0.836516303737469, 0.22414386804185735, -0.12940952255092145],
    [
        0.3326705529509569,
        0.8068915093133388,
        0.4598775021193313,
        -0.13501102001039084,
        -0.08544127388224149,
        0.035226291882100656,
    ],
    [
        0.23037781330885523,
        0.7148465705525415,
        0.6308807679295904,
        -0.02798376941698385,
        -0.18703481171888114,
        0.030841381835986965,
        0.032883011666982945,
        -0.010597401784997278,
    ],
    [
        0.160102397974125,
        0.6038292697974729,
        0.7243085284385744,
        0.13842814590110342,
        -0.24229488706619015,
        -0.03224486958502952,
        0.07757149384006515,
        -0.006241490213011705,
        -0.012580751999015526,
        0.003335725285001549,
    ],
    [
        0.11154074335008017,
        0.4946238903983854,
        0.7511339080215775,
        0.3152503517092432,
        -0.22626469396516913,
        -0.12976686756709563,
        0.09750160558707936,
        0.02752286553001629,
        -0.031582039318031156,
        0.0005538422009938016,
        0.004777257511010651,
        -0.00107730108499558,
    ],
    [
        0.07785205408506236,
        0.39653931948230575,
        0.7291320908465551,
        0.4697822874053586,
        -0.14390600392910627,
        -0.22403618499416572,
        0.07130921926705004,
        0.0806126091510659,
        -0.03802993693503463,
        -0.01657454163101562,
        0.012550998556013784,
        0.00042957797300470274,
        -0.0018016407039998328,
        0.0003537138000010399,
    ],
    [
        0.05441584224308161,
        0.3128715909144659,
        0.6756307362980128,
        0.5853546836548691,
        -0.015829105256023893,
        -0.2840155429624281,
        0.00047248457399797254,
        0.128747426620186,
        -0.01736930100202211,
        -0.04408825393106472,
        0.013981027917015516,
        0.008746094047015655,
        -0.00487035299301066,
        -0.0003917403729959771,
        0.0006754494059985568,
        -0.00011747678400228192,
    ],
]


def tap_pairs(basis):
    taps = np.array(daubechies_table[basis])
    low = taps / np.sum(taps)
    high = np.array([(-1.0) ** t * low[len(low) - 1 - t] for t in range(len(low))])
    return low, high


def composite(basis):
    low, high = tap_pairs(basis)
    n = len(low) // 2
    fine = [{t - n: f[t] for t in range(2 * n)} for f in (low, high)]
    both = []
    for f in (low, high):
        out = {}
        for s in range(2 * n):
            for t in range(2 * n):
                off = (s - n) + 2 * (t - n)
                out[off] = out.get(off, 0.0) + low[s] * f[t]
        both.append(out)
    return fine + both


def halves(matrix):
    high = matrix.astype(np.float32).astype(ml_dtypes.bfloat16)
    low = (matrix - high.astype(np.float64)).astype(np.float32).astype(ml_dtypes.bfloat16)
    return np.stack([high, low])


@functools.lru_cache(maxsize=None)
def matrices(h, w):
    span = h + 2 * REACH
    scale = 1.0 / math.sqrt(BASES)
    a = np.zeros((BASES, 4 * span, 2 * h))
    b = np.zeros((BASES, BANDS * h, span))
    c = np.zeros((BASES, 8, 2 * w), np.float32)
    kinds = [(1, 0), (0, 1), (1, 1), (3, 2), (2, 3), (3, 3), (2, 2)]
    for basis in range(BASES):
        filters = composite(basis)
        rows = np.zeros((4, h, span))
        for kind in range(4):
            for off, tap in filters[kind].items():
                for j in range(h):
                    rows[kind, j, j + REACH + off] += scale * tap
                c[basis, kind, off % (2 * w)] += tap
        for band, (row_kind, col_kind) in enumerate(kinds):
            mat = rows[row_kind]
            at = COLUMN_BANDS[col_kind].index(band)
            a[basis, col_kind * span : (col_kind + 1) * span, at * h : (at + 1) * h] = mat.T
            place = BAND_ORDER.index(band)
            b[basis, place * h : (place + 1) * h] = mat
    return halves(a), halves(b), c


def split(x):
    high = x.astype(jnp.bfloat16)
    low = (x - high.astype(jnp.float32)).astype(jnp.bfloat16)
    return high, low


def column_matrix(c_ref, k, w):
    parts = []
    for kind in range(4):
        first = jnp.broadcast_to(c_ref[k, kind : kind + 1], (w, 2 * w))
        parts.append(pltpu.roll(first, 0, 1, stride=1, stride_axis=0))
    return split(jnp.concatenate(parts, axis=0))


def left_dot(m_high, m_low, x):
    width = x.shape[1]
    high, low = split(x)
    pair = jnp.dot(
        m_high, jnp.concatenate([high, low], axis=1), preferred_element_type=jnp.float32
    )
    rest = jnp.dot(m_low, high, preferred_element_type=jnp.float32)
    return pair[:, :width] + (pair[:, width:] + rest)


def synth_one(x_ref, a_ref, c_ref, k, h, w):
    span = h + 2 * REACH
    parts = []
    for kind, bands in enumerate(COLUMN_BANDS):
        rows, depth = slice(kind * span, (kind + 1) * span), len(bands) * h
        data = [x_ref[k, band * h : (band + 1) * h] for band in bands]
        data = jnp.concatenate(data, axis=0) if len(data) > 1 else data[0]
        parts.append(left_dot(a_ref[0, k, rows, :depth], a_ref[1, k, rows, :depth], data))
    z = jnp.concatenate(parts, axis=1)
    high, low = split(z)
    c_high, c_low = column_matrix(c_ref, k, w)
    pair = jnp.dot(
        jnp.concatenate([high, low], axis=0), c_high, preferred_element_type=jnp.float32
    )
    rest = jnp.dot(high, c_low, preferred_element_type=jnp.float32)
    return pair[:span] + (pair[span:] + rest)


def partners():
    return [(dr, dc) for dr in (-2, -1, 0, 1, 2) for dc in (-1, 0, 1) if (dr, dc) != (0, 0)]


def near():
    return [(dr, dc) for dr in (-1, 0, 1) for dc in (-1, 0, 1) if (dr, dc) != (0, 0)]


def overlap(dr, h):
    span = h + 2 * REACH
    shift = h * abs(dr)
    return (shift, 0, span - shift) if dr > 0 else (0, shift, span - shift)


def border(dr, h):
    if dr == 0:
        return (REACH, REACH, h)
    return (h, 0, REACH) if dr > 0 else (REACH, h + REACH, REACH)


def primal_kernel(
    it_ref, gr_ref, x_ref, a_ref, c_ref, e_ref, img_ref,
    acc, held, slots, side, sides_in, bar_sent, bar_recv, send, recv,
):
    h, w = it_ref.shape
    span = h + 2 * REACH
    step = pl.program_id(0)
    nrow, ncol = lax.axis_size("row"), lax.axis_size("col")
    row, col = lax.axis_index("row"), lax.axis_index("col")

    def device(dr, dc):
        return (lax.rem(row + dr + 2 * nrow, nrow), lax.rem(col + dc + ncol, ncol))

    def held_copy(i, dr, dc):
        here, there, rows = border(dr, h)
        return pltpu.make_async_remote_copy(
            src_ref=held.at[1, pl.ds(here, rows)],
            dst_ref=held.at[1 + dc if dc else 3, pl.ds(there, rows)],
            send_sem=bar_sent.at[i], recv_sem=bar_recv.at[i],
            device_id=device(dr, dc), device_id_type=MESH,
        )

    def sum_copy(i, dr, dc):
        here, there, rows = overlap(dr, h)
        slot = dr + 2
        if dc == 0:
            src = acc.at[pl.ds(here, rows)]
            dst = slots.at[slot, pl.ds(there, rows)]
        else:
            src = side.at[(dc + 1) // 2, pl.ds(here, rows)]
            dst = sides_in.at[(dc + 1) // 2, slot, pl.ds(there, rows)]
        return pltpu.make_async_remote_copy(
            src_ref=src, dst_ref=dst, send_sem=send.at[i], recv_sem=recv.at[i],
            device_id=device(dr, dc), device_id_type=MESH,
        )

    @pl.when(step == 0)
    def _():
        barrier = pltpu.get_barrier_semaphore()
        for dr, dc in partners():
            pl.semaphore_signal(barrier, inc=1, device_id=device(dr, dc), device_id_type=MESH)
        held[1, REACH : REACH + h] = it_ref[...]
        acc[...] = jnp.zeros_like(acc)
        acc[REACH : REACH + h, :w] = it_ref[...] - primal_step * gr_ref[...]

    @pl.when(step == 1)
    def _():
        pl.semaphore_wait(pltpu.get_barrier_semaphore(), len(partners()))
        for i, (dr, dc) in enumerate(near()):
            held_copy(i, dr, dc).start()

    total = synth_one(x_ref, a_ref, c_ref, 0, h, w)
    for k in range(1, GROUP):
        total = total + synth_one(x_ref, a_ref, c_ref, k, h, w)
    acc[...] += -primal_step * total

    @pl.when(step == BASES // GROUP - 1)
    def _():
        left = lax.broadcasted_iota(jnp.int32, (span, w), 1) < w // 2
        mine, over = acc[:, :w], acc[:, w:]
        side[0] = jnp.where(left, mine, over)
        side[1] = jnp.where(left, over, mine)
        for i, (dr, dc) in enumerate(partners()):
            sum_copy(i, dr, dc).start()
        for i, (dr, dc) in enumerate(near()):
            held_copy(i, dr, dc).wait()
        for i, (dr, dc) in enumerate(partners()):
            sum_copy(i, dr, dc).wait()

        def gather(read, start):
            total = start
            for dr in (-2, -1, 0, 1, 2):
                if dr == 0 and start is not None:
                    continue
                _, there, rows = overlap(dr, h)
                part = read(dr + 2, there, rows)
                sizes = (there, span - there - rows)
                above, below = [jnp.zeros((n, part.shape[1]), jnp.float32) for n in sizes]
                blocks = [above] * (there > 0) + [part] + [below] * (sizes[1] > 0)
                part = jnp.concatenate(blocks, axis=0) if len(blocks) > 1 else part
                total = part if total is None else total + part
            return total

        mid = gather(lambda s, t, n: slots[s, t : t + n], acc[...])
        from_right = gather(lambda s, t, n: sides_in[0, s, t : t + n], None)
        from_left = gather(lambda s, t, n: sides_in[1, s, t : t + n], None)
        inner = mid[:, :w] + jnp.where(left, from_left, from_right)
        outer = mid[:, w:] + jnp.where(left, from_right, from_left)
        inner = jnp.maximum(inner, 0.0)
        outer = jnp.maximum(outer, 0.0)
        img_ref[...] = inner[REACH : REACH + h]
        it_inner = jnp.concatenate(
            [held[3, :REACH], held[1, REACH : REACH + h], held[3, REACH + h :]], axis=0
        )
        it_outer = jnp.where(left, held[0], held[2])
        ext = jnp.concatenate([2.0 * inner - it_inner, 2.0 * outer - it_outer], axis=1)
        high, low = split(ext)
        e_ref[:span] = high
        e_ref[span:] = low


def dual_kernel(wt_ref, e_ref, img_ref, x_ref, b_ref, c_ref, img_out, x_out):
    h, w = img_ref.shape
    span = h + 2 * REACH
    step = pl.program_id(0)

    @pl.when(step == 0)
    def _():
        img_out[...] = img_ref[...]

    across = (((1,), (1,)), ((), ()))
    for k in range(GROUP):
        c_high, c_low = column_matrix(c_ref, k, w)
        pair = lax.dot_general(
            e_ref[...], c_high, across, preferred_element_type=jnp.float32
        )
        rest = lax.dot_general(
            e_ref[:span], c_low, across, preferred_element_type=jnp.float32
        )
        z = pair[:span] + (pair[span:] + rest)
        done = 0
        for kind, bands in enumerate(COLUMN_BANDS):
            rows = slice(done * h, (done + len(bands)) * h)
            done += len(bands)
            data = z[:, kind * w : (kind + 1) * w]
            coeffs = left_dot(b_ref[0, k, rows], b_ref[1, k, rows], data)
            for at, band in enumerate(bands):
                bound = wt_ref[step * GROUP + k, band]
                value = x_ref[k, band * h : (band + 1) * h] + coeffs[at * h : (at + 1) * h]
                x_out[k, band * h : (band + 1) * h] = jnp.clip(value, -bound, bound)


def on_device(iterate, gradient, dual_coeffs, weights):
    h, w = iterate.shape
    span = h + 2 * REACH
    a, b, c = [jnp.asarray(m) for m in matrices(h, w)]
    duals = dual_coeffs.reshape(BASES, BANDS * h, w)
    whole = pl.BlockSpec((h, w), lambda i: (0, 0))
    per_basis = pl.BlockSpec((GROUP, BANDS * h, w), lambda i: (i, 0, 0))
    first_rows = pl.BlockSpec((GROUP, 8, 2 * w), lambda i: (i, 0, 0))
    halved = lambda m: pl.BlockSpec((2, GROUP) + m.shape[2:], lambda i: (0, i, 0, 0))
    ext, image = pl.pallas_call(
        primal_kernel,
        grid=(BASES // GROUP,),
        out_shape=(
            jax.ShapeDtypeStruct((2 * span, 2 * w), jnp.bfloat16),
            jax.ShapeDtypeStruct((h, w), jnp.float32),
        ),
        in_specs=[whole, whole, per_basis, halved(a), first_rows],
        out_specs=(pl.BlockSpec((2 * span, 2 * w), lambda i: (0, 0)), whole),
        scratch_shapes=[
            pltpu.VMEM((span, 2 * w), jnp.float32),
            pltpu.VMEM((4, span, w), jnp.float32),
            pltpu.VMEM((5, span, 2 * w), jnp.float32),
            pltpu.VMEM((2, span, w), jnp.float32),
            pltpu.VMEM((2, 5, span, w), jnp.float32),
            pltpu.SemaphoreType.DMA((8,)),
            pltpu.SemaphoreType.DMA((8,)),
            pltpu.SemaphoreType.DMA((14,)),
            pltpu.SemaphoreType.DMA((14,)),
        ],
        compiler_params=pltpu.CompilerParams(
            collective_id=0, has_side_effects=True, vmem_limit_bytes=VMEM_LIMIT
        ),
    )(iterate, gradient, duals, a, c)
    new_image, new_duals = pl.pallas_call(
        dual_kernel,
        grid=(BASES // GROUP,),
        out_shape=(
            jax.ShapeDtypeStruct((h, w), jnp.float32),
            jax.ShapeDtypeStruct(duals.shape, jnp.float32),
        ),
        in_specs=[
            pl.BlockSpec(memory_space=pltpu.SMEM),
            pl.BlockSpec((2 * span, 2 * w), lambda i: (0, 0)),
            whole,
            per_basis,
            halved(b),
            first_rows,
        ],
        out_specs=(whole, per_basis),
        compiler_params=pltpu.CompilerParams(vmem_limit_bytes=VMEM_LIMIT),
    )(weights, ext, image, duals, b, c)
    return new_image, new_duals.reshape(dual_coeffs.shape)


def solution(mesh):
    return jax.shard_map(
        on_device,
        mesh=mesh,
        in_specs=(P("row", "col"), P("row", "col"), P(None, None, "row", "col"), P()),
        out_specs=(P("row", "col"), P(None, None, "row", "col")),
        check_vma=False,
    )
```

```python
import functools
import math

import jax
import jax.numpy as jnp
import ml_dtypes
import numpy as np
from jax import lax
from jax.experimental import pallas as pl
from jax.experimental.pallas import tpu as pltpu
from jax.sharding import PartitionSpec as P

BASES = 8
BANDS = 7
REACH = 24
GROUP = 4
VMEM_LIMIT = 24 * 2**20
COLUMN_BANDS = [(0,), (1, 2), (3, 6), (4, 5)]
BAND_ORDER = [0, 1, 2, 3, 6, 4, 5]
MESH = pl.DeviceIdType.MESH

primal_step = 0.5

daubechies_table = [
    [0.7071067811865476, 0.7071067811865476],
    [0.48296291314469025, 0.836516303737469, 0.22414386804185735, -0.12940952255092145],
    [
        0.3326705529509569,
        0.8068915093133388,
        0.4598775021193313,
        -0.13501102001039084,
        -0.08544127388224149,
        0.035226291882100656,
    ],
    [
        0.23037781330885523,
        0.7148465705525415,
        0.6308807679295904,
        -0.02798376941698385,
        -0.18703481171888114,
        0.030841381835986965,
        0.032883011666982945,
        -0.010597401784997278,
    ],
    [
        0.160102397974125,
        0.6038292697974729,
        0.7243085284385744,
        0.13842814590110342,
        -0.24229488706619015,
        -0.03224486958502952,
        0.07757149384006515,
        -0.006241490213011705,
        -0.012580751999015526,
        0.003335725285001549,
    ],
    [
        0.11154074335008017,
        0.4946238903983854,
        0.7511339080215775,
        0.3152503517092432,
        -0.22626469396516913,
        -0.12976686756709563,
        0.09750160558707936,
        0.02752286553001629,
        -0.031582039318031156,
        0.0005538422009938016,
        0.004777257511010651,
        -0.00107730108499558,
    ],
    [
        0.07785205408506236,
        0.39653931948230575,
        0.7291320908465551,
        0.4697822874053586,
        -0.14390600392910627,
        -0.22403618499416572,
        0.07130921926705004,
        0.0806126091510659,
        -0.03802993693503463,
        -0.01657454163101562,
        0.012550998556013784,
        0.00042957797300470274,
        -0.0018016407039998328,
        0.0003537138000010399,
    ],
    [
        0.05441584224308161,
        0.3128715909144659,
        0.6756307362980128,
        0.5853546836548691,
        -0.015829105256023893,
        -0.2840155429624281,
        0.00047248457399797254,
        0.128747426620186,
        -0.01736930100202211,
        -0.04408825393106472,
        0.013981027917015516,
        0.008746094047015655,
        -0.00487035299301066,
        -0.0003917403729959771,
        0.0006754494059985568,
        -0.00011747678400228192,
    ],
]


def tap_pairs(basis):
    taps = np.array(daubechies_table[basis])
    low = taps / np.sum(taps)
    high = np.array([(-1.0) ** t * low[len(low) - 1 - t] for t in range(len(low))])
    return low, high


def composite(basis):
    low, high = tap_pairs(basis)
    n = len(low) // 2
    fine = [{t - n: f[t] for t in range(2 * n)} for f in (low, high)]
    both = []
    for f in (low, high):
        out = {}
        for s in range(2 * n):
            for t in range(2 * n):
                off = (s - n) + 2 * (t - n)
                out[off] = out.get(off, 0.0) + low[s] * f[t]
        both.append(out)
    return fine + both


def halves(matrix):
    high = matrix.astype(np.float32).astype(ml_dtypes.bfloat16)
    low = (matrix - high.astype(np.float64)).astype(np.float32).astype(ml_dtypes.bfloat16)
    return np.stack([high, low])


@functools.lru_cache(maxsize=None)
def matrices(h, w):
    span = h + 2 * REACH
    scale = 1.0 / math.sqrt(BASES)
    a = np.zeros((BASES, 4 * span, 2 * h))
    b = np.zeros((BASES, BANDS * h, span))
    c = np.zeros((BASES, 8, 2 * w), np.float32)
    kinds = [(1, 0), (0, 1), (1, 1), (3, 2), (2, 3), (3, 3), (2, 2)]
    for basis in range(BASES):
        filters = composite(basis)
        rows = np.zeros((4, h, span))
        for kind in range(4):
            for off, tap in filters[kind].items():
                for j in range(h):
                    rows[kind, j, j + REACH + off] += scale * tap
                c[basis, kind, off % (2 * w)] += tap
        for band, (row_kind, col_kind) in enumerate(kinds):
            mat = rows[row_kind]
            at = COLUMN_BANDS[col_kind].index(band)
            a[basis, col_kind * span : (col_kind + 1) * span, at * h : (at + 1) * h] = mat.T
            place = BAND_ORDER.index(band)
            b[basis, place * h : (place + 1) * h] = mat
    return halves(a), halves(b), c


def split(x):
    high = x.astype(jnp.bfloat16)
    low = (x - high.astype(jnp.float32)).astype(jnp.bfloat16)
    return high, low


def column_matrix(c_ref, k, w):
    parts = []
    for kind in range(4):
        first = jnp.broadcast_to(c_ref[k, kind : kind + 1], (w, 2 * w))
        parts.append(pltpu.roll(first, 0, 1, stride=1, stride_axis=0))
    return split(jnp.concatenate(parts, axis=0))


def left_dot(m_high, m_low, x):
    width = x.shape[1]
    high, low = split(x)
    pair = jnp.dot(
        m_high, jnp.concatenate([high, low], axis=1), preferred_element_type=jnp.float32
    )
    rest = jnp.dot(m_low, high, preferred_element_type=jnp.float32)
    return pair[:, :width] + (pair[:, width:] + rest)


def synth_one(x_ref, a_ref, c_ref, k, h, w):
    span = h + 2 * REACH
    parts = []
    for kind, bands in enumerate(COLUMN_BANDS):
        rows, depth = slice(kind * span, (kind + 1) * span), len(bands) * h
        data = [x_ref[k, band * h : (band + 1) * h] for band in bands]
        data = jnp.concatenate(data, axis=0) if len(data) > 1 else data[0]
        parts.append(left_dot(a_ref[0, k, rows, :depth], a_ref[1, k, rows, :depth], data))
    z = jnp.concatenate(parts, axis=1)
    high, low = split(z)
    c_high, c_low = column_matrix(c_ref, k, w)
    pair = jnp.dot(
        jnp.concatenate([high, low], axis=0), c_high, preferred_element_type=jnp.float32
    )
    rest = jnp.dot(high, c_low, preferred_element_type=jnp.float32)
    return pair[:span] + (pair[span:] + rest)


def partners():
    return [(dr, dc) for dr in (-2, -1, 0, 1, 2) for dc in (-1, 0, 1) if (dr, dc) != (0, 0)]


def near():
    return [(dr, dc) for dr in (-1, 0, 1) for dc in (-1, 0, 1) if (dr, dc) != (0, 0)]


def overlap(dr, h):
    span = h + 2 * REACH
    shift = h * abs(dr)
    return (shift, 0, span - shift) if dr > 0 else (0, shift, span - shift)


def border(dr, h):
    if dr == 0:
        return (REACH, REACH, h)
    return (h, 0, REACH) if dr > 0 else (REACH, h + REACH, REACH)


def primal_kernel(
    it_ref, gr_ref, x_ref, a_ref, c_ref, e_ref, img_ref,
    acc, held, slots, side, sides_in, bar_sent, bar_recv, send, recv,
):
    h, w = it_ref.shape
    span = h + 2 * REACH
    step = pl.program_id(0)
    nrow, ncol = lax.axis_size("row"), lax.axis_size("col")
    row, col = lax.axis_index("row"), lax.axis_index("col")

    def device(dr, dc):
        return (lax.rem(row + dr + 2 * nrow, nrow), lax.rem(col + dc + ncol, ncol))

    def held_copy(i, dr, dc):
        here, there, rows = border(dr, h)
        return pltpu.make_async_remote_copy(
            src_ref=held.at[1, pl.ds(here, rows)],
            dst_ref=held.at[1 + dc if dc else 3, pl.ds(there, rows)],
            send_sem=bar_sent.at[i], recv_sem=bar_recv.at[i],
            device_id=device(dr, dc), device_id_type=MESH,
        )

    def sum_copy(i, dr, dc):
        here, there, rows = overlap(dr, h)
        slot = dr + 2
        if dc == 0:
            src = acc.at[pl.ds(here, rows)]
            dst = slots.at[slot, pl.ds(there, rows)]
        else:
            src = side.at[(dc + 1) // 2, pl.ds(here, rows)]
            dst = sides_in.at[(dc + 1) // 2, slot, pl.ds(there, rows)]
        return pltpu.make_async_remote_copy(
            src_ref=src, dst_ref=dst, send_sem=send.at[i], recv_sem=recv.at[i],
            device_id=device(dr, dc), device_id_type=MESH,
        )

    @pl.when(step == 0)
    def _():
        barrier = pltpu.get_barrier_semaphore()
        for dr, dc in partners():
            pl.semaphore_signal(barrier, inc=1, device_id=device(dr, dc), device_id_type=MESH)
        held[1, REACH : REACH + h] = it_ref[...]
        acc[...] = jnp.zeros_like(acc)
        acc[REACH : REACH + h, :w] = it_ref[...] - primal_step * gr_ref[...]

    @pl.when(step == 1)
    def _():
        pl.semaphore_wait(pltpu.get_barrier_semaphore(), len(partners()))
        for i, (dr, dc) in enumerate(near()):
            held_copy(i, dr, dc).start()

    total = synth_one(x_ref, a_ref, c_ref, 0, h, w)
    for k in range(1, GROUP):
        total = total + synth_one(x_ref, a_ref, c_ref, k, h, w)
    acc[...] += -primal_step * total

    @pl.when(step == BASES // GROUP - 1)
    def _():
        left = lax.broadcasted_iota(jnp.int32, (span, w), 1) < w // 2
        mine, over = acc[:, :w], acc[:, w:]
        side[0] = jnp.where(left, mine, over)
        side[1] = jnp.where(left, over, mine)
        for i, (dr, dc) in enumerate(partners()):
            sum_copy(i, dr, dc).start()
        for i, (dr, dc) in enumerate(near()):
            held_copy(i, dr, dc).wait()
        for i, (dr, dc) in enumerate(partners()):
            sum_copy(i, dr, dc).wait()

        def gather(read, start):
            total = start
            for dr in (-2, -1, 0, 1, 2):
                if dr == 0 and start is not None:
                    continue
                _, there, rows = overlap(dr, h)
                part = read(dr + 2, there, rows)
                sizes = (there, span - there - rows)
                above, below = [jnp.zeros((n, part.shape[1]), jnp.float32) for n in sizes]
                blocks = [above] * (there > 0) + [part] + [below] * (sizes[1] > 0)
                part = jnp.concatenate(blocks, axis=0) if len(blocks) > 1 else part
                total = part if total is None else total + part
            return total

        mid = gather(lambda s, t, n: slots[s, t : t + n], acc[...])
        from_right = gather(lambda s, t, n: sides_in[0, s, t : t + n], None)
        from_left = gather(lambda s, t, n: sides_in[1, s, t : t + n], None)
        inner = mid[:, :w] + jnp.where(left, from_left, from_right)
        outer = mid[:, w:] + jnp.where(left, from_right, from_left)
        inner = jnp.maximum(inner, 0.0)
        outer = jnp.maximum(outer, 0.0)
        img_ref[...] = inner[REACH : REACH + h]
        it_inner = jnp.concatenate(
            [held[3, :REACH], held[1, REACH : REACH + h], held[3, REACH + h :]], axis=0
        )
        it_outer = jnp.where(left, held[0], held[2])
        ext = jnp.concatenate([2.0 * inner - it_inner, 2.0 * outer - it_outer], axis=1)
        high, low = split(ext)
        e_ref[:span] = high
        e_ref[span:] = low


def dual_kernel(wt_ref, e_ref, img_ref, x_ref, b_ref, c_ref, img_out, x_out):
    h, w = img_ref.shape
    span = h + 2 * REACH
    step = pl.program_id(0)

    @pl.when(step == 0)
    def _():
        img_out[...] = img_ref[...]

    across = (((1,), (1,)), ((), ()))
    for k in range(GROUP):
        c_high, c_low = column_matrix(c_ref, k, w)
        pair = lax.dot_general(
            e_ref[...], c_high, across, preferred_element_type=jnp.float32
        )
        rest = lax.dot_general(
            e_ref[:span], c_low, across, preferred_element_type=jnp.float32
        )
        z = pair[:span] + (pair[span:] + rest)
        done = 0
        for kind, bands in enumerate(COLUMN_BANDS):
            rows = slice(done * h, (done + len(bands)) * h)
            done += len(bands)
            data = z[:, kind * w : (kind + 1) * w]
            coeffs = left_dot(b_ref[0, k, rows], b_ref[1, k, rows], data)
            for at, band in enumerate(bands):
                bound = wt_ref[step * GROUP + k, band]
                value = x_ref[k, band * h : (band + 1) * h] + coeffs[at * h : (at + 1) * h]
                x_out[k, band * h : (band + 1) * h] = jnp.clip(value, -bound, bound)


def on_device(iterate, gradient, dual_coeffs, weights):
    h, w = iterate.shape
    span = h + 2 * REACH
    a, b, c = [jnp.asarray(m) for m in matrices(h, w)]
    duals = dual_coeffs.reshape(BASES, BANDS * h, w)
    whole = pl.BlockSpec((h, w), lambda i: (0, 0))
    per_basis = pl.BlockSpec((GROUP, BANDS * h, w), lambda i: (i, 0, 0))
    first_rows = pl.BlockSpec((GROUP, 8, 2 * w), lambda i: (i, 0, 0))
    halved = lambda m: pl.BlockSpec((2, GROUP) + m.shape[2:], lambda i: (0, i, 0, 0))
    ext, image = pl.pallas_call(
        primal_kernel,
        grid=(BASES // GROUP,),
        out_shape=(
            jax.ShapeDtypeStruct((2 * span, 2 * w), jnp.bfloat16),
            jax.ShapeDtypeStruct((h, w), jnp.float32),
        ),
        in_specs=[whole, whole, per_basis, halved(a), first_rows],
        out_specs=(pl.BlockSpec((2 * span, 2 * w), lambda i: (0, 0)), whole),
        scratch_shapes=[
            pltpu.VMEM((span, 2 * w), jnp.float32),
            pltpu.VMEM((4, span, w), jnp.float32),
            pltpu.VMEM((5, span, 2 * w), jnp.float32),
            pltpu.VMEM((2, span, w), jnp.float32),
            pltpu.VMEM((2, 5, span, w), jnp.float32),
            pltpu.SemaphoreType.DMA((8,)),
            pltpu.SemaphoreType.DMA((8,)),
            pltpu.SemaphoreType.DMA((14,)),
            pltpu.SemaphoreType.DMA((14,)),
        ],
        compiler_params=pltpu.CompilerParams(
            collective_id=0, has_side_effects=True, vmem_limit_bytes=VMEM_LIMIT
        ),
    )(iterate, gradient, duals, a, c)
    new_image, new_duals = pl.pallas_call(
        dual_kernel,
        grid=(BASES // GROUP,),
        out_shape=(
            jax.ShapeDtypeStruct((h, w), jnp.float32),
            jax.ShapeDtypeStruct(duals.shape, jnp.float32),
        ),
        in_specs=[
            pl.BlockSpec(memory_space=pltpu.SMEM),
            pl.BlockSpec((2 * span, 2 * w), lambda i: (0, 0)),
            whole,
            per_basis,
            halved(b),
            first_rows,
        ],
        out_specs=(whole, per_basis),
        compiler_params=pltpu.CompilerParams(vmem_limit_bytes=VMEM_LIMIT),
    )(weights, ext, image, duals, b, c)
    return new_image, new_duals.reshape(dual_coeffs.shape)


def solution(mesh):
    return jax.shard_map(
        on_device,
        mesh=mesh,
        in_specs=(P("row", "col"), P("row", "col"), P(None, None, "row", "col"), P()),
        out_specs=(P("row", "col"), P(None, None, "row", "col")),
        check_vma=False,
    )
```

```python
import functools
import math

import jax
import jax.numpy as jnp
import ml_dtypes
import numpy as np
from jax import lax
from jax.experimental import pallas as pl
from jax.experimental.pallas import tpu as pltpu
from jax.sharding import PartitionSpec as P

BASES = 8
BANDS = 7
REACH = 24
GROUP = 4
VMEM_LIMIT = 24 * 2**20
COLUMN_BANDS = [(0,), (1, 2), (3, 6), (4, 5)]
BAND_ORDER = [0, 1, 2, 3, 6, 4, 5]
MESH = pl.DeviceIdType.MESH

primal_step = 0.5

daubechies_table = [
    [0.7071067811865476, 0.7071067811865476],
    [0.48296291314469025, 0.836516303737469, 0.22414386804185735, -0.12940952255092145],
    [
        0.3326705529509569,
        0.8068915093133388,
        0.4598775021193313,
        -0.13501102001039084,
        -0.08544127388224149,
        0.035226291882100656,
    ],
    [
        0.23037781330885523,
        0.7148465705525415,
        0.6308807679295904,
        -0.02798376941698385,
        -0.18703481171888114,
        0.030841381835986965,
        0.032883011666982945,
        -0.010597401784997278,
    ],
    [
        0.160102397974125,
        0.6038292697974729,
        0.7243085284385744,
        0.13842814590110342,
        -0.24229488706619015,
        -0.03224486958502952,
        0.07757149384006515,
        -0.006241490213011705,
        -0.012580751999015526,
        0.003335725285001549,
    ],
    [
        0.11154074335008017,
        0.4946238903983854,
        0.7511339080215775,
        0.3152503517092432,
        -0.22626469396516913,
        -0.12976686756709563,
        0.09750160558707936,
        0.02752286553001629,
        -0.031582039318031156,
        0.0005538422009938016,
        0.004777257511010651,
        -0.00107730108499558,
    ],
    [
        0.07785205408506236,
        0.39653931948230575,
        0.7291320908465551,
        0.4697822874053586,
        -0.14390600392910627,
        -0.22403618499416572,
        0.07130921926705004,
        0.0806126091510659,
        -0.03802993693503463,
        -0.01657454163101562,
        0.012550998556013784,
        0.00042957797300470274,
        -0.0018016407039998328,
        0.0003537138000010399,
    ],
    [
        0.05441584224308161,
        0.3128715909144659,
        0.6756307362980128,
        0.5853546836548691,
        -0.015829105256023893,
        -0.2840155429624281,
        0.00047248457399797254,
        0.128747426620186,
        -0.01736930100202211,
        -0.04408825393106472,
        0.013981027917015516,
        0.008746094047015655,
        -0.00487035299301066,
        -0.0003917403729959771,
        0.0006754494059985568,
        -0.00011747678400228192,
    ],
]


def tap_pairs(basis):
    taps = np.array(daubechies_table[basis])
    low = taps / np.sum(taps)
    high = np.array([(-1.0) ** t * low[len(low) - 1 - t] for t in range(len(low))])
    return low, high


def composite(basis):
    low, high = tap_pairs(basis)
    n = len(low) // 2
    fine = [{t - n: f[t] for t in range(2 * n)} for f in (low, high)]
    both = []
    for f in (low, high):
        out = {}
        for s in range(2 * n):
            for t in range(2 * n):
                off = (s - n) + 2 * (t - n)
                out[off] = out.get(off, 0.0) + low[s] * f[t]
        both.append(out)
    return fine + both


def halves(matrix):
    high = matrix.astype(np.float32).astype(ml_dtypes.bfloat16)
    low = (matrix - high.astype(np.float64)).astype(np.float32).astype(ml_dtypes.bfloat16)
    return np.stack([high, low])


@functools.lru_cache(maxsize=None)
def matrices(h, w):
    span = h + 2 * REACH
    scale = 1.0 / math.sqrt(BASES)
    a = np.zeros((BASES, 4 * span, 2 * h))
    b = np.zeros((BASES, BANDS * h, span))
    c = np.zeros((BASES, 8, 2 * w), np.float32)
    kinds = [(1, 0), (0, 1), (1, 1), (3, 2), (2, 3), (3, 3), (2, 2)]
    for basis in range(BASES):
        filters = composite(basis)
        rows = np.zeros((4, h, span))
        for kind in range(4):
            for off, tap in filters[kind].items():
                for j in range(h):
                    rows[kind, j, j + REACH + off] += scale * tap
                c[basis, kind, off % (2 * w)] += tap
        for band, (row_kind, col_kind) in enumerate(kinds):
            mat = rows[row_kind]
            at = COLUMN_BANDS[col_kind].index(band)
            a[basis, col_kind * span : (col_kind + 1) * span, at * h : (at + 1) * h] = mat.T
            place = BAND_ORDER.index(band)
            b[basis, place * h : (place + 1) * h] = mat
    return halves(a), halves(b), c


def split(x):
    high = x.astype(jnp.bfloat16)
    low = (x - high.astype(jnp.float32)).astype(jnp.bfloat16)
    return high, low


def column_matrix(c_ref, k, w):
    parts = []
    for kind in range(4):
        first = jnp.broadcast_to(c_ref[k, kind : kind + 1], (w, 2 * w))
        parts.append(pltpu.roll(first, 0, 1, stride=1, stride_axis=0))
    return split(jnp.concatenate(parts, axis=0))


def left_dot(m_high, m_low, x):
    width = x.shape[1]
    high, low = split(x)
    pair = jnp.dot(
        m_high, jnp.concatenate([high, low], axis=1), preferred_element_type=jnp.float32
    )
    rest = jnp.dot(m_low, high, preferred_element_type=jnp.float32)
    return pair[:, :width] + (pair[:, width:] + rest)


def synth_one(x_ref, a_ref, c_ref, k, h, w):
    span = h + 2 * REACH
    parts = []
    for kind, bands in enumerate(COLUMN_BANDS):
        rows, depth = slice(kind * span, (kind + 1) * span), len(bands) * h
        data = [x_ref[k, band * h : (band + 1) * h] for band in bands]
        data = jnp.concatenate(data, axis=0) if len(data) > 1 else data[0]
        parts.append(left_dot(a_ref[0, k, rows, :depth], a_ref[1, k, rows, :depth], data))
    z = jnp.concatenate(parts, axis=1)
    high, low = split(z)
    c_high, c_low = column_matrix(c_ref, k, w)
    pair = jnp.dot(
        jnp.concatenate([high, low], axis=0), c_high, preferred_element_type=jnp.float32
    )
    rest = jnp.dot(high, c_low, preferred_element_type=jnp.float32)
    return pair[:span] + (pair[span:] + rest)


def partners():
    return [(dr, dc) for dr in (-2, -1, 0, 1, 2) for dc in (-1, 0, 1) if (dr, dc) != (0, 0)]


def near():
    return [(dr, dc) for dr in (-1, 0, 1) for dc in (-1, 0, 1) if (dr, dc) != (0, 0)]


def overlap(dr, h):
    span = h + 2 * REACH
    shift = h * abs(dr)
    return (shift, 0, span - shift) if dr > 0 else (0, shift, span - shift)


def border(dr, h):
    if dr == 0:
        return (REACH, REACH, h)
    return (h, 0, REACH) if dr > 0 else (REACH, h + REACH, REACH)


def primal_kernel(
    it_ref, gr_ref, x_ref, a_ref, c_ref, e_ref, img_ref,
    acc, held, slots, side, sides_in, bar_sent, bar_recv, send, recv,
):
    h, w = it_ref.shape
    span = h + 2 * REACH
    step = pl.program_id(0)
    nrow, ncol = lax.axis_size("row"), lax.axis_size("col")
    row, col = lax.axis_index("row"), lax.axis_index("col")

    def device(dr, dc):
        return (lax.rem(row + dr + 2 * nrow, nrow), lax.rem(col + dc + ncol, ncol))

    def held_copy(i, dr, dc):
        here, there, rows = border(dr, h)
        return pltpu.make_async_remote_copy(
            src_ref=held.at[1, pl.ds(here, rows)],
            dst_ref=held.at[1 + dc if dc else 3, pl.ds(there, rows)],
            send_sem=bar_sent.at[i], recv_sem=bar_recv.at[i],
            device_id=device(dr, dc), device_id_type=MESH,
        )

    def sum_copy(i, dr, dc):
        here, there, rows = overlap(dr, h)
        slot = dr + 2
        if dc == 0:
            src = acc.at[pl.ds(here, rows)]
            dst = slots.at[slot, pl.ds(there, rows)]
        else:
            src = side.at[(dc + 1) // 2, pl.ds(here, rows)]
            dst = sides_in.at[(dc + 1) // 2, slot, pl.ds(there, rows)]
        return pltpu.make_async_remote_copy(
            src_ref=src, dst_ref=dst, send_sem=send.at[i], recv_sem=recv.at[i],
            device_id=device(dr, dc), device_id_type=MESH,
        )

    @pl.when(step == 0)
    def _():
        barrier = pltpu.get_barrier_semaphore()
        for dr, dc in partners():
            pl.semaphore_signal(barrier, inc=1, device_id=device(dr, dc), device_id_type=MESH)
        held[1, REACH : REACH + h] = it_ref[...]
        acc[...] = jnp.zeros_like(acc)
        acc[REACH : REACH + h, :w] = it_ref[...] - primal_step * gr_ref[...]

    @pl.when(step == 1)
    def _():
        pl.semaphore_wait(pltpu.get_barrier_semaphore(), len(partners()))
        for i, (dr, dc) in enumerate(near()):
            held_copy(i, dr, dc).start()

    total = synth_one(x_ref, a_ref, c_ref, 0, h, w)
    for k in range(1, GROUP):
        total = total + synth_one(x_ref, a_ref, c_ref, k, h, w)
    acc[...] += -primal_step * total

    @pl.when(step == BASES // GROUP - 1)
    def _():
        left = lax.broadcasted_iota(jnp.int32, (span, w), 1) < w // 2
        mine, over = acc[:, :w], acc[:, w:]
        side[0] = jnp.where(left, mine, over)
        side[1] = jnp.where(left, over, mine)
        for i, (dr, dc) in enumerate(partners()):
            sum_copy(i, dr, dc).start()
        for i, (dr, dc) in enumerate(near()):
            held_copy(i, dr, dc).wait()
        for i, (dr, dc) in enumerate(partners()):
            sum_copy(i, dr, dc).wait()

        def gather(read, start):
            total = start
            for dr in (-2, -1, 0, 1, 2):
                if dr == 0 and start is not None:
                    continue
                _, there, rows = overlap(dr, h)
                part = read(dr + 2, there, rows)
                sizes = (there, span - there - rows)
                above, below = [jnp.zeros((n, part.shape[1]), jnp.float32) for n in sizes]
                blocks = [above] * (there > 0) + [part] + [below] * (sizes[1] > 0)
                part = jnp.concatenate(blocks, axis=0) if len(blocks) > 1 else part
                total = part if total is None else total + part
            return total

        mid = gather(lambda s, t, n: slots[s, t : t + n], acc[...])
        from_right = gather(lambda s, t, n: sides_in[0, s, t : t + n], None)
        from_left = gather(lambda s, t, n: sides_in[1, s, t : t + n], None)
        inner = mid[:, :w] + jnp.where(left, from_left, from_right)
        outer = mid[:, w:] + jnp.where(left, from_right, from_left)
        inner = jnp.maximum(inner, 0.0)
        outer = jnp.maximum(outer, 0.0)
        img_ref[...] = inner[REACH : REACH + h]
        it_inner = jnp.concatenate(
            [held[3, :REACH], held[1, REACH : REACH + h], held[3, REACH + h :]], axis=0
        )
        it_outer = jnp.where(left, held[0], held[2])
        ext = jnp.concatenate([2.0 * inner - it_inner, 2.0 * outer - it_outer], axis=1)
        high, low = split(ext)
        e_ref[:span] = high
        e_ref[span:] = low


def dual_kernel(wt_ref, e_ref, img_ref, x_ref, b_ref, c_ref, img_out, x_out):
    h, w = img_ref.shape
    span = h + 2 * REACH
    step = pl.program_id(0)

    @pl.when(step == 0)
    def _():
        img_out[...] = img_ref[...]

    across = (((1,), (1,)), ((), ()))
    for k in range(GROUP):
        c_high, c_low = column_matrix(c_ref, k, w)
        pair = lax.dot_general(
            e_ref[...], c_high, across, preferred_element_type=jnp.float32
        )
        rest = lax.dot_general(
            e_ref[:span], c_low, across, preferred_element_type=jnp.float32
        )
        z = pair[:span] + (pair[span:] + rest)
        done = 0
        for kind, bands in enumerate(COLUMN_BANDS):
            rows = slice(done * h, (done + len(bands)) * h)
            done += len(bands)
            data = z[:, kind * w : (kind + 1) * w]
            coeffs = left_dot(b_ref[0, k, rows], b_ref[1, k, rows], data)
            for at, band in enumerate(bands):
                bound = wt_ref[step * GROUP + k, band]
                value = x_ref[k, band * h : (band + 1) * h] + coeffs[at * h : (at + 1) * h]
                x_out[k, band * h : (band + 1) * h] = jnp.clip(value, -bound, bound)


def on_device(iterate, gradient, dual_coeffs, weights):
    h, w = iterate.shape
    span = h + 2 * REACH
    a, b, c = [jnp.asarray(m) for m in matrices(h, w)]
    duals = dual_coeffs.reshape(BASES, BANDS * h, w)
    whole = pl.BlockSpec((h, w), lambda i: (0, 0))
    per_basis = pl.BlockSpec((GROUP, BANDS * h, w), lambda i: (i, 0, 0))
    first_rows = pl.BlockSpec((GROUP, 8, 2 * w), lambda i: (i, 0, 0))
    halved = lambda m: pl.BlockSpec((2, GROUP) + m.shape[2:], lambda i: (0, i, 0, 0))
    ext, image = pl.pallas_call(
        primal_kernel,
        grid=(BASES // GROUP,),
        out_shape=(
            jax.ShapeDtypeStruct((2 * span, 2 * w), jnp.bfloat16),
            jax.ShapeDtypeStruct((h, w), jnp.float32),
        ),
        in_specs=[whole, whole, per_basis, halved(a), first_rows],
        out_specs=(pl.BlockSpec((2 * span, 2 * w), lambda i: (0, 0)), whole),
        scratch_shapes=[
            pltpu.VMEM((span, 2 * w), jnp.float32),
            pltpu.VMEM((4, span, w), jnp.float32),
            pltpu.VMEM((5, span, 2 * w), jnp.float32),
            pltpu.VMEM((2, span, w), jnp.float32),
            pltpu.VMEM((2, 5, span, w), jnp.float32),
            pltpu.SemaphoreType.DMA((8,)),
            pltpu.SemaphoreType.DMA((8,)),
            pltpu.SemaphoreType.DMA((14,)),
            pltpu.SemaphoreType.DMA((14,)),
        ],
        compiler_params=pltpu.CompilerParams(
            collective_id=0, has_side_effects=True, vmem_limit_bytes=VMEM_LIMIT
        ),
    )(*[pltpu.with_memory_space_constraint(x, pltpu.HBM) for x in (iterate, gradient, duals, a, c)])
    new_image, new_duals = pl.pallas_call(
        dual_kernel,
        grid=(BASES // GROUP,),
        out_shape=(
            jax.ShapeDtypeStruct((h, w), jnp.float32),
            jax.ShapeDtypeStruct(duals.shape, jnp.float32),
        ),
        in_specs=[
            pl.BlockSpec(memory_space=pltpu.SMEM),
            pl.BlockSpec((2 * span, 2 * w), lambda i: (0, 0)),
            whole,
            per_basis,
            halved(b),
            first_rows,
        ],
        out_specs=(whole, per_basis),
        compiler_params=pltpu.CompilerParams(vmem_limit_bytes=VMEM_LIMIT),
    )(weights, ext, image, duals, b, c)
    return new_image, new_duals.reshape(dual_coeffs.shape)


def solution(mesh):
    return jax.shard_map(
        on_device,
        mesh=mesh,
        in_specs=(P("row", "col"), P("row", "col"), P(None, None, "row", "col"), P()),
        out_specs=(P("row", "col"), P(None, None, "row", "col")),
        check_vma=False,
    )
```
